128 devices in a mesh: dp: 4 (over z), expert: 32 (over y, x, core).
Axes of the slice: x: 4, y: 4, z: 4, core: 2. Of those that a mesh axis runs over, the one named last changes fastest.
Arguments:
- tokens: bfloat16 [3072, 4096], P(('dp', 'expert')), may hold values from -6 to 6
- out_grad: bfloat16 [3072, 4096], P(('dp', 'expert')), may hold values from -1.5 to 1.5
- routes: int32 [3072, 8], P(('dp', 'expert')), may hold values from 0 to 63, all different within a row; in each aligned block of 24 rows (0 to 23, 24 to 47, ...) at most 6 rows name the same one
- gate_probs: bfloat16 [3072, 8], P(('dp', 'expert')), may hold values from 0.049804688 to 0.29882812
- gate_weight: bfloat16 [128, 4096, 384], P(('dp', 'expert')), may hold values from -0.09375 to 0.09375
- up_weight: bfloat16 [128, 4096, 384], P(('dp', 'expert')), may hold values from -0.09375 to 0.09375
- down_weight: bfloat16 [128, 384, 4096], P(('dp', 'expert')), may hold values from -0.21875 to 0.21875
Outputs:
- token_grad: bfloat16 [3072, 4096], P(('dp', 'expert'))
- prob_grad: float32 [3072, 8], P(('dp', 'expert'))
- gate_grad: bfloat16 [128, 4096, 384], P(('dp', 'expert'))
- up_grad: bfloat16 [128, 4096, 384], P(('dp', 'expert'))
- down_grad: bfloat16 [128, 384, 4096], P(('dp', 'expert'))
The draws below stay inside these ranges and needn't reach their ends.
Inputs may be any that keep to these rules, and one draw needn't show every extreme that they name: `routes`: each token names 8 different experts; in the rows of one device no expert is named by more than 6 slots, a bound that some block reaches of them.
All inputs are finite; a program needn't handle non-finite values.
Results may differ from the reference program's by a relative error of at most 0.0057.
Values may be sent and summed in bfloat16 or wider, within the bound.
A program may use at most 192 MiB of HBM per device.

```python
import math
import jax
import jax.numpy as jnp
import numpy as np
from jax import lax

D = 4096
FF = 768
TOP = 8
TOK_DEV = 24
HALF = 384
EXPERTS = 64
CAP = 6
TOKENS = 3072
N_DP = 4
N_EXPERT = 32


def block_scale(key, shape, pieces, smallest, high):
    loudness = 1.0
    for axis_at, parts in pieces:
        draws = jax.random.uniform(jax.random.fold_in(jax.random.fold_in(key, 6), axis_at), (parts,), jnp.float32, smallest / len(pieces), high / len(pieces))
        loudness = loudness * jnp.repeat(jnp.exp(draws), shape[axis_at] // parts).reshape((-1,) + (1,) * (len(shape) - 1 - axis_at))
    return loudness


def deal_out(stream_key, own, number, rows, number_of, top, bound, lean):
    order = jax.random.permutation(stream_key, number_of)
    crowded, ordinary = shares(number_of, rows * top, bound, lean, True), shares(number_of, rows * top, bound, lean, False)
    places = jnp.arange(number_of)

    def named(tallies, turn):
        used = int((tallies > 0).sum())
        fixed = max(1, used // 4)
        passed = fixed + (places - fixed + turn * (used - fixed)) % max(1, number_of - fixed)
        return jnp.zeros((number_of,), jnp.int32).at[order[jnp.where(places < fixed, places, passed)]].set(jnp.asarray(tallies, jnp.int32))

    tallies = jnp.where(number % 4 == 0, named(crowded, number // 4), named(ordinary, number - number // 4 - 1))
    mixed = jax.random.permutation(jax.random.fold_in(own, 3), number_of)
    giver, sink = mixed[0:number_of // 2 * 2:2], mixed[1:number_of // 2 * 2:2]
    slack = jnp.minimum(tallies[giver] - 1, bound - tallies[sink]) // 2
    slack = jnp.where((giver == order[0]) | (sink == order[0]) | (tallies[sink] == 0), 0, jnp.maximum(slack, 0))
    passed = jax.random.randint(jax.random.fold_in(own, 4), (number_of // 2,), 0, 1 << 20) % (slack + 1)
    tallies = tallies.at[giver].add(-passed).at[sink].add(passed)
    items = jnp.searchsorted(jnp.cumsum(tallies), jnp.arange(rows * top), side="right").astype(jnp.int32)
    grid = items.reshape(top, rows).T
    grid = grid[jax.random.permutation(jax.random.fold_in(own, 1), rows)]
    turn = jax.random.randint(jax.random.fold_in(own, 2), (rows, 1), 0, top)
    return jnp.take_along_axis(grid, (jnp.arange(top)[None, :] + turn) % top, axis=1)


def shares(count, total, limit, skew, full):
    portions = [(1 << 20) // math.isqrt(rank ** skew) + 1 for rank in range(1, count + 1)]
    largest = limit if full else min(limit, max(-(-total // count), total * portions[0] // sum(portions)))
    least = 1 if total - largest >= count - 1 else 0
    given, surplus = [largest] + [least] * (count - 1), total - largest - least * (count - 1)
    while surplus > 0:
        free = [i for i in range(1, count) if given[i] < largest] or [i for i in range(1, count) if given[i] < limit]
        pool, budget = sum([portions[i] for i in free]), surplus
        for i in free:
            addition = min(limit - given[i], max(1, budget * portions[i] // pool), surplus)
            given[i] = given[i] + addition
            surplus = surplus - addition
    return np.array(given)


def normal_values(own_key, dims, deviation, reach, cuts=(), kind=jnp.bfloat16):
    loudness = block_scale(own_key, dims, cuts, -0.22, 0.18) if cuts else 1.0
    result = jax.random.normal(own_key, dims, jnp.float32) * deviation * loudness
    return jnp.minimum(jnp.maximum(result, -reach), reach).astype(kind)


def setup_inputs(seed: int = 0) -> dict:
    keys = jax.random.split(jax.random.key(seed), 8)
    tokens = normal_values(keys[0], (TOKENS, D), 1.0, 6.0, ((0, 128),))
    out_grad = normal_values(keys[1], (TOKENS, D), 0.25, 1.5, ((0, 128),))
    routes_keys = jax.random.split(jax.random.fold_in(keys[2], 1), TOKENS // TOK_DEV)
    routes_turns = jax.random.permutation(jax.random.fold_in(keys[2], 3), TOKENS // TOK_DEV)
    routes = jax.vmap(lambda own, number: deal_out(jax.random.fold_in(keys[2], 2), own, number, TOK_DEV, EXPERTS, TOP, CAP, 2))(routes_keys, routes_turns).reshape((TOKENS, TOP))
    gate_probs = jnp.clip(0.049804688 + 0.24902344 * jax.random.uniform(keys[3], (TOKENS, TOP), jnp.float32) ** block_scale(keys[3], (TOKENS, TOP), ((0, 128),), -0.2, 0.2), 0.049804688, 0.29882812).astype(jnp.bfloat16)
    gate_weight = normal_values(keys[4], (2 * EXPERTS, D, HALF), D ** -0.5, 0.09375, ((0, 128),))
    up_weight = normal_values(keys[5], (2 * EXPERTS, D, HALF), D ** -0.5, 0.09375, ((0, 128),))
    down_weight = normal_values(keys[6], (2 * EXPERTS, HALF, D), FF ** -0.5, 0.21875, ((0, 128),))
    return {"tokens": tokens, "out_grad": out_grad, "routes": routes, "gate_probs": gate_probs, "gate_weight": gate_weight, "up_weight": up_weight, "down_weight": down_weight}


def half_terms(rows_in, grads_in, probs_in, gate_half, up_half, down_half):
    gate_pre = jnp.dot(rows_in, gate_half, preferred_element_type=jnp.float32)
    up_pre = jnp.dot(rows_in, up_half, preferred_element_type=jnp.float32)
    sigmoid = jax.nn.sigmoid(gate_pre)
    active = gate_pre * sigmoid
    hidden = active * up_pre
    raw_grad = jnp.dot(grads_in, down_half.T, preferred_element_type=jnp.float32)
    prob_part = jnp.sum(hidden * raw_grad, axis=1).astype(jnp.bfloat16)
    weight = probs_in.astype(jnp.float32)[:, None]
    scaled_grad = weight * raw_grad
    gate_delta = (scaled_grad * up_pre * sigmoid * (1.0 + gate_pre * (1.0 - sigmoid))).astype(jnp.bfloat16)
    up_delta = (scaled_grad * active).astype(jnp.bfloat16)
    scaled_hidden = (weight * hidden).astype(jnp.bfloat16)
    gate_sum = jnp.dot(rows_in.T, gate_delta, preferred_element_type=jnp.float32)
    up_sum = jnp.dot(rows_in.T, up_delta, preferred_element_type=jnp.float32)
    down_sum = jnp.dot(scaled_hidden.T, grads_in, preferred_element_type=jnp.float32)
    input_part = (jnp.dot(gate_delta, gate_half.T, preferred_element_type=jnp.float32)
                  + jnp.dot(up_delta, up_half.T, preferred_element_type=jnp.float32)).astype(jnp.bfloat16)
    return gate_sum, up_sum, down_sum, input_part, prob_part


def reference(tokens, out_grad, routes, gate_probs, gate_weight, up_weight, down_weight):
    device_count = N_DP * N_EXPERT
    slot_count = TOK_DEV * TOP
    chosen = routes.reshape(device_count, slot_count).astype(jnp.int32)
    labels = jnp.arange(EXPERTS, dtype=jnp.int32)
    onehot = (chosen[:, :, None] == labels[None, None, :]).astype(jnp.int32)
    slot_rank = jnp.sum((jnp.cumsum(onehot, axis=1).astype(jnp.int32) - onehot) * onehot, axis=2).astype(jnp.int32)
    slot_ids = jnp.arange(device_count * slot_count, dtype=jnp.int32).reshape(device_count, slot_count)
    sources = jnp.broadcast_to(jnp.arange(device_count, dtype=jnp.int32)[:, None], (device_count, slot_count))
    slot_table = jnp.full((EXPERTS, device_count, CAP), -1, dtype=jnp.int32)
    slot_table = slot_table.at[chosen, sources, slot_rank].set(slot_ids).reshape(EXPERTS, device_count * CAP)
    probs_flat = gate_probs.reshape(TOKENS * TOP).astype(jnp.float32)
    gate_pairs = gate_weight.reshape(EXPERTS, 2, D, HALF)
    up_pairs = up_weight.reshape(EXPERTS, 2, D, HALF)
    down_pairs = down_weight.reshape(EXPERTS, 2, HALF, D)

    def expert_step(totals, inputs):
        input_sum, prob_sum = totals
        slots, gate_pair, up_pair, down_pair = inputs
        occupied = slots >= 0
        safe_slot = jnp.where(occupied, slots, 0).astype(jnp.int32)
        token_index = (safe_slot // TOP).astype(jnp.int32)
        rows_in = tokens[token_index]
        grads_in = out_grad[token_index]
        probs_in = jnp.where(occupied, probs_flat[safe_slot], 0.0)
        gate_list, up_list, down_list = [], [], []
        for half_index in range(2):
            gate_sum, up_sum, down_sum, input_part, prob_part = half_terms(
                rows_in, grads_in, probs_in, gate_pair[half_index], up_pair[half_index], down_pair[half_index])
            input_sum = input_sum.at[token_index].add(jnp.where(occupied[:, None], input_part.astype(jnp.float32), 0.0))
            prob_sum = prob_sum.at[safe_slot].add(jnp.where(occupied, prob_part.astype(jnp.float32), 0.0))
            gate_list.append(gate_sum.astype(jnp.bfloat16))
            up_list.append(up_sum.astype(jnp.bfloat16))
            down_list.append(down_sum.astype(jnp.bfloat16))
        return (input_sum, prob_sum), (jnp.stack(gate_list), jnp.stack(up_list), jnp.stack(down_list))

    start_carry = (jnp.zeros((TOKENS, D), jnp.float32), jnp.zeros((TOKENS * TOP,), jnp.float32))
    (input_sum, prob_sum), (gate_stack, up_stack, down_stack) = lax.scan(
        expert_step, start_carry, (slot_table, gate_pairs, up_pairs, down_pairs))
    return (input_sum.astype(jnp.bfloat16), prob_sum.reshape(TOKENS, TOP),
            gate_stack.reshape(2 * EXPERTS, D, HALF), up_stack.reshape(2 * EXPERTS, D, HALF),
            down_stack.reshape(2 * EXPERTS, HALF, D))
```

```python
import numpy as np
import jax
import jax.numpy as jnp
from jax import lax
from jax.sharding import PartitionSpec as P
from jax.experimental import pallas as pl
from jax.experimental.pallas import tpu as pltpu

MESH = pl.DeviceIdType.MESH
D = 4096
HALF = 384
TOK = 24
TOP = 8
CAP = 6
RING = 4
SLOTS = 16 * CAP
CLASS = RING * SLOTS
BLOCK = 2 * TOK
PLANE = 16 * BLOCK
X, Y, Z = 0, 1, 2
ORDERS = ((Z, Y, X), (X, Z, Y), (Y, X, Z))
FWD = ((0, 1408), (1408, 1408), (2816, 1280))
WIDE = (1536, 1536, 1408)
SENT = 1408
BACK = ((0, 1536), (1536, 1280), (2816, 1280))
BACK_WIDE = (1536, 1280, 1536)


def place_tables():
    i = np.arange(CLASS)
    x, y, z, r = i // 96, i // 24 % 4, i // 6 % 4, i % 6
    rows = (y * 96 + (z * 4 + x) * 6 + r, z * 96 + (x * 4 + y) * 6 + r)
    perm = np.stack([(np.arange(CLASS)[None, :] == w[:, None]) for w in rows]).astype(np.float32)
    k = np.arange(PLANE)
    seg = np.stack([k // BLOCK * CAP, k % BLOCK // TOK]).astype(np.float32)
    return perm, seg


PERM, SEG = place_tables()


def position():
    dp, ex = lax.axis_index("dp"), lax.axis_index("expert")
    return (lax.rem(ex // 2, 4), ex // 8, dp), lax.rem(ex, 2)


def device(co, core):
    return (co[2], co[1] * 8 + co[0] * 2 + core)


def shifted(co, axis, by):
    out = list(co)
    out[axis] = lax.rem(co[axis] + by, RING)
    return tuple(out)


def enter(co, core):
    barrier = pltpu.get_barrier_semaphore()
    for axis in (X, Y, Z):
        for by in (1, 2, 3):
            pl.semaphore_signal(
                barrier, inc=1, device_id=device(shifted(co, axis, by), core), device_id_type=MESH
            )
    pl.semaphore_signal(barrier, inc=1, device_id=device(co, 1 - core), device_id_type=MESH)
    pl.semaphore_wait(barrier, 10)


def remote(src, dst, send, recv, to):
    return pltpu.make_async_remote_copy(
        src_ref=src, dst_ref=dst, send_sem=send, recv_sem=recv, device_id=to, device_id_type=MESH
    )


def expert_of(co):
    return co[2] * 16 + co[1] * 4 + co[0]


def rows_at(start, size):
    return pl.ds(pl.multiple_of(start, 16), size)


def dispatch_kernel(
    tok, grd, routes, probs, perm, seg,
    rows_t, rows_g, picked, metas,
    g0, g1, g2, s0, s1, s2, r0, r1, r2, st_t, st_g, st_m,
    a1_s, a1_r, a2_s, a2_r, x_s, x_r, d_s, d_r, l_s,
):
    co, core = position()
    gs, ss, rs = (g0, g1, g2), (s0, s1, s2), (r0, r1, r2)
    enter(co, core)

    lane = lax.broadcasted_iota(jnp.int32, (TOK, 128), 1)
    named = jnp.zeros((TOK, 128), jnp.float32)
    weight = jnp.zeros((TOK, 128), jnp.float32)
    for k in range(TOP):
        route = routes[:, k:k + 1]
        named = named + jnp.where(lane == route, 1.0, 0.0)
        weight = weight + jnp.where(lane == route + 64, probs[:, k:k + 1].astype(jnp.float32), 0.0)
    before = lax.broadcasted_iota(jnp.int32, (TOK, TOK), 0) > lax.broadcasted_iota(
        jnp.int32, (TOK, TOK), 1
    )
    rank = jnp.dot(
        jnp.where(before, 1.0, 0.0), named, preferred_element_type=jnp.float32
    )
    meta = named * (rank + 1.0) + weight
    meta = jnp.concatenate([meta, meta], axis=0).astype(jnp.bfloat16)

    a1_in = []
    for p, (a1, a2, a3) in enumerate(ORDERS):
        at, wide = FWD[p]
        mine = rows_at((co[a2] * 4 + co[a1]) * BLOCK, BLOCK)
        both = jnp.concatenate(
            [tok[:, at:at + wide].astype(jnp.float32), grd[:, at:at + wide].astype(jnp.float32)], axis=0
        )
        gs[p][mine, 0:wide] = both.astype(jnp.bfloat16)
        gs[p][mine, wide:wide + 128] = meta
    outs = []
    for by in (1, 3, 2):
        for p, (a1, a2, a3) in enumerate(ORDERS):
            mine = rows_at((co[a2] * 4 + co[a1]) * BLOCK, BLOCK)
            c = remote(
                gs[p].at[mine], gs[p].at[mine], a1_s.at[p, by - 1], a1_r.at[p, by - 1],
                device(shifted(co, a1, by), core),
            )
            c.start()
            outs.append(c)
            theirs = rows_at((co[a2] * 4 + lax.rem(co[a1] + 4 - by, 4)) * BLOCK, BLOCK)
            a1_in.append((p, gs[p].at[theirs], a1_s.at[p, by - 1], a1_r.at[p, by - 1]))

    def arrive(ref, send, recv):
        remote(ref, ref, send, recv, device(shifted(co, X, 1), core)).wait_recv()

    def half(p, b, which):
        return gs[p].at[rows_at(b * 192 + which * 96, 96)]

    for p, (a1, a2, a3) in enumerate(ORDERS):
        for q, ref, s, r in a1_in:
            if q == p:
                arrive(ref, s, r)
    for p, (a1, a2, a3) in enumerate(ORDERS):
        up, down = device(shifted(co, a2, 1), core), device(shifted(co, a2, 3), core)
        for idx, which, to in ((0, 0, up), (3, 1, down), (1, 1, up), (4, 0, down)):
            ref = half(p, co[a2], which)
            c = remote(ref, ref, a2_s.at[p, idx], a2_r.at[p, idx], to)
            c.start()
            outs.append(c)
    for p, (a1, a2, a3) in enumerate(ORDERS):
        up, down = device(shifted(co, a2, 1), core), device(shifted(co, a2, 3), core)
        for got, idx, by, which, to in ((0, 2, 3, 0, up), (3, 5, 1, 1, down)):
            ref = half(p, lax.rem(co[a2] + by, 4), which)
            arrive(ref, a2_s.at[p, got], a2_r.at[p, got])
            c = remote(ref, ref, a2_s.at[p, idx], a2_r.at[p, idx], to)
            c.start()
            outs.append(c)
    for p, (a1, a2, a3) in enumerate(ORDERS):
        for idx, by, which in ((1, 3, 1), (4, 1, 0), (2, 2, 0), (5, 2, 1)):
            arrive(half(p, lax.rem(co[a2] + by, 4), which), a2_s.at[p, idx], a2_r.at[p, idx])

    tg = seg[1:2, :]
    wants = []
    for p, (a1, a2, a3) in enumerate(ORDERS):
        wide = WIDE[p]
        tile = gs[p][:, wide - 128:wide]
        metas[p] = tile
        line = lax.broadcasted_iota(jnp.int32, (8, 128), 0)
        lane8 = lax.broadcasted_iota(jnp.int32, (8, 128), 1)
        name = jnp.full((8, 128), -1, jnp.int32)
        for by in range(4):
            name = jnp.where(line == by, expert_of(shifted(co, a3, by)), name)
        pick = jnp.where(lane8 == name, 1.0, 0.0).astype(jnp.bfloat16)
        val = lax.dot_general(
            pick, tile, (((1,), (1,)), ((), ())), preferred_element_type=jnp.float32
        )
        wants.append(jnp.where(val > 0.5, val - 1.0 + seg[0:1, :], -1.0))
    slot = lax.broadcasted_iota(jnp.int32, (SLOTS, PLANE), 0).astype(jnp.float32)
    for by in (1, 3, 2, 0):
        for p, (a1, a2, a3) in enumerate(ORDERS):
            want = wants[p][by:by + 1, :]
            choose = jnp.concatenate(
                [
                    jnp.where(slot == jnp.where(tg < 0.5, want, -1.0), 1.0, 0.0),
                    jnp.where(slot == jnp.where(tg > 0.5, want, -1.0), 1.0, 0.0),
                ],
                axis=0,
            ).astype(jnp.bfloat16)
            got = jnp.dot(
                choose, gs[p][:, 0:SENT],
                preferred_element_type=jnp.float32,
            ).astype(jnp.bfloat16)
            if by == 0:
                rs[p][rows_at(co[a3] * 192, 192), :] = got
            else:
                ss[p][by - 1] = got
                c = remote(
                    ss[p].at[by - 1], rs[p].at[rows_at(co[a3] * 192, 192)],
                    x_s.at[p, by - 1], x_r.at[p, by - 1], device(shifted(co, a3, by), core),
                )
                c.start()
                outs.append(c)

    partner = device(co, 1 - core)
    locals_ = []
    for p, (a1, a2, a3) in enumerate(ORDERS):
        for by in (1, 3, 2):
            ref = rs[p].at[rows_at(lax.rem(co[a3] + 4 - by, 4) * 192, 192)]
            arrive(ref, x_s.at[p, by - 1], x_r.at[p, by - 1])
        at, wide = FWD[p]
        for half_at, stage, out, n in ((0, st_t, rows_t, 0), (96, st_g, rows_g, 1)):
            full = jnp.concatenate(
                [rs[p][b * 192 + half_at:b * 192 + half_at + 96, :] for b in range(4)], axis=0
            )
            if p > 0:
                full = jnp.dot(perm[p - 1], full, preferred_element_type=jnp.float32).astype(
                    jnp.bfloat16
                )
            stage[:, at:at + wide] = full[:, 0:wide]
            jobs = [(stage.at[:, at:at + wide], out.at[core, :, at:at + wide], n)]
            if p == 2 and n == 0:
                st_m[...] = full[:, wide:wide + 128]
                jobs.append((st_m, picked.at[core], 2))
            for src, dst, m in jobs:
                c = remote(src, dst, d_s.at[p, m], d_r.at[p, m], partner)
                c.start()
                outs.append(c)
                c = pltpu.make_async_copy(src, dst, l_s.at[p, m])
                c.start()
                locals_.append(c)
    for p in range(3):
        at, wide = FWD[p]
        jobs = [(rows_t.at[1 - core, :, at:at + wide], 0), (rows_g.at[1 - core, :, at:at + wide], 1)]
        if p == 2:
            jobs.append((picked.at[1 - core], 2))
        for ref, m in jobs:
            arrive(ref, d_s.at[p, m], d_r.at[p, m])
    for c in outs:
        c.wait_send()
    for c in locals_:
        c.wait()


def dispatch(tokens, out_grad, routes, gate_probs):
    vmem = pl.BlockSpec(memory_space=pltpu.VMEM)
    anywhere = pl.BlockSpec(memory_space=pl.ANY)
    bf = jnp.bfloat16
    dma = pltpu.SemaphoreType.DMA
    return pl.pallas_call(
        dispatch_kernel,
        out_shape=(
            jax.ShapeDtypeStruct((2, CLASS, D), bf),
            jax.ShapeDtypeStruct((2, CLASS, D), bf),
            jax.ShapeDtypeStruct((2, CLASS, 128), bf),
            jax.ShapeDtypeStruct((3, PLANE, 128), bf),
        ),
        in_specs=[vmem] * 6,
        out_specs=(anywhere, anywhere, anywhere, vmem),
        scratch_shapes=[pltpu.VMEM((PLANE, w), bf) for w in WIDE]
        + [pltpu.VMEM((3, 192, SENT), bf) for _ in range(3)]
        + [pltpu.VMEM((4 * 192, SENT), bf) for _ in range(3)]
        + [pltpu.VMEM((CLASS, D), bf), pltpu.VMEM((CLASS, D), bf), pltpu.VMEM((CLASS, 128), bf)]
        + [dma((3, 3)), dma((3, 3)), dma((3, 6)), dma((3, 6)), dma((3, 3)), dma((3, 3))]
        + [dma((3, 3)), dma((3, 3)), dma((3, 3))],
        compiler_params=pltpu.CompilerParams(
            collective_id=1, has_side_effects=True, vmem_limit_bytes=56 * 2**20
        ),
        name="dispatch",
    )(
        tokens, out_grad, routes, gate_probs,
        jnp.asarray(PERM, jnp.bfloat16), jnp.asarray(SEG, jnp.float32),
    )


def combine_kernel(
    parts, probs, metas, routes, perm_t, seg,
    token_grad, prob_grad,
    mine, other, mine_p, other_p, s0, s1, s2, r0, r1, r2, t0, t1, t2,
    b0, b1, b2, u0, u1, u2, c0, c1, c2,
    d_s, d_r, l_s, x_s, x_r, a2_s, a2_r, a1_s, a1_r,
):
    co, core = position()
    ss, rs, ts = (s0, s1, s2), (r0, r1, r2), (t0, t1, t2)
    bs, us, cs = (b0, b1, b2), (u0, u1, u2), (c0, c1, c2)
    enter(co, core)
    partner = device(co, 1 - core)
    outs = []

    def arrive(ref, send, recv):
        remote(ref, ref, send, recv, partner).wait_recv()

    def send(src, dst, s, r, to):
        c = remote(src, dst, s, r, to)
        c.start()
        outs.append(c)

    for p in range(3):
        at, wide = BACK[p]
        send(
            parts.at[1 - core, :, at:at + wide], other.at[:, at:at + wide],
            d_s.at[p], d_r.at[p], partner,
        )
    send(probs.at[1 - core], other_p, d_s.at[3], d_r.at[3], partner)
    own = pltpu.make_async_copy(parts.at[core], mine, l_s.at[0])
    own.start()
    own_p = pltpu.make_async_copy(probs.at[core], mine_p, l_s.at[1])
    own_p.start()
    own.wait()
    own_p.wait()
    arrive(other_p, d_s.at[3], d_r.at[3])
    lane = lax.broadcasted_iota(jnp.int32, (CLASS, 128), 1)
    prob = jnp.where(lane == expert_of(co), mine_p[...] + other_p[...], 0.0)
    prob_hi = prob.astype(jnp.bfloat16)
    prob_lo = (prob - prob_hi.astype(jnp.float32)).astype(jnp.bfloat16)

    for p, (a1, a2, a3) in enumerate(ORDERS):
        at, wide = BACK[p]
        arrive(other.at[:, at:at + wide], d_s.at[p], d_r.at[p])
        both = (
            mine[:, at:at + wide].astype(jnp.float32) + other[:, at:at + wide].astype(jnp.float32)
        ).astype(jnp.bfloat16)
        if p == 2:
            both = jnp.concatenate([both, prob_hi, prob_lo], axis=1)
        if p > 0:
            both = jnp.dot(perm_t[p - 1], both, preferred_element_type=jnp.float32).astype(
                jnp.bfloat16
            )
        ss[p][...] = both
        for by in (1, 3, 2):
            to = shifted(co, a3, by)
            send(
                ss[p].at[rows_at(to[a3] * SLOTS, SLOTS)], rs[p].at[rows_at(co[a3] * SLOTS, SLOTS)],
                x_s.at[p, by - 1], x_r.at[p, by - 1], device(to, core),
            )
        rs[p][rows_at(co[a3] * SLOTS, SLOTS), :] = ss[p][rows_at(co[a3] * SLOTS, SLOTS), :]

    code = lax.broadcasted_iota(jnp.int32, (PLANE, 2 * CLASS), 1).astype(jnp.float32)
    for p, (a1, a2, a3) in enumerate(ORDERS):
        h = BACK_WIDE[p] // 2
        line = lax.broadcasted_iota(jnp.int32, (128, 128), 0)
        lane = lax.broadcasted_iota(jnp.int32, (128, 128), 1)
        name = jnp.full((128, 128), -1, jnp.int32)
        for b in range(4):
            at_b = list(co)
            at_b[a3] = b
            name = jnp.where(line == b, expert_of(at_b), name)
        pick = jnp.where(lane == name, 1.0, 0.0).astype(jnp.bfloat16)
        val = lax.dot_general(
            metas[p], pick, (((1,), (1,)), ((), ())), preferred_element_type=jnp.float32
        )
        lane = lax.broadcasted_iota(jnp.int32, (PLANE, 128), 1).astype(jnp.float32)
        spot = jnp.where(val > 0.5, val - 1.0 + seg[0] + lane * SLOTS + seg[1] * CLASS, -1.0)
        put = jnp.zeros((PLANE, 2 * CLASS), jnp.float32)
        for b in range(4):
            put = jnp.where(code == spot[:, b:b + 1], 1.0, put)
        put = put.astype(jnp.bfloat16)
        for by in (1, 3, 2):
            ref = rs[p].at[rows_at(lax.rem(co[a3] + 4 - by, 4) * SLOTS, SLOTS)]
            arrive(ref, x_s.at[p, by - 1], x_r.at[p, by - 1])
        stacked = jnp.concatenate([rs[p][:, 0:h], rs[p][:, h:2 * h]], axis=0)
        ts[p][...] = jnp.dot(put, stacked, preferred_element_type=jnp.float32).astype(jnp.bfloat16)
        for by in (1, 3, 2):
            to = shifted(co, a2, by)
            send(
                ts[p].at[rows_at(to[a2] * 192, 192)], bs[p].at[by - 1],
                a2_s.at[p, by - 1], a2_r.at[p, by - 1], device(to, core),
            )
    for p, (a1, a2, a3) in enumerate(ORDERS):
        total = ts[p][rows_at(co[a2] * 192, 192), :].astype(jnp.float32)
        for by in (1, 3, 2):
            arrive(bs[p].at[by - 1], a2_s.at[p, by - 1], a2_r.at[p, by - 1])
            total = total + bs[p][by - 1].astype(jnp.float32)
        us[p][...] = total.astype(jnp.bfloat16)
        for by in (1, 3, 2):
            to = shifted(co, a1, by)
            send(
                us[p].at[rows_at(to[a1] * BLOCK, BLOCK)], cs[p].at[by - 1],
                a1_s.at[p, by - 1], a1_r.at[p, by - 1], device(to, core),
            )
    for p, (a1, a2, a3) in enumerate(ORDERS):
        total = us[p][rows_at(co[a1] * BLOCK, BLOCK), :].astype(jnp.float32)
        for by in (1, 3, 2):
            arrive(cs[p].at[by - 1], a1_s.at[p, by - 1], a1_r.at[p, by - 1])
            total = total + cs[p][by - 1].astype(jnp.float32)
        at, wide = BACK[p]
        h = BACK_WIDE[p] // 2
        token_grad[:, at:at + h] = total[0:TOK].astype(jnp.bfloat16)
        rest = wide - h
        token_grad[:, at + h:at + wide] = total[TOK:, 0:rest].astype(jnp.bfloat16)
        if p == 2:
            per = total[TOK:, rest:rest + 128] + total[TOK:, rest + 128:rest + 256]
            lane = lax.broadcasted_iota(jnp.int32, (TOK, 128), 1)
            spot = lax.broadcasted_iota(jnp.int32, (TOK, TOP), 1)
            grad = jnp.zeros((TOK, TOP), jnp.float32)
            for k in range(TOP):
                one = jnp.sum(jnp.where(lane == routes[:, k:k + 1], per, 0.0), axis=1, keepdims=True)
                grad = jnp.where(spot == k, one, grad)
            prob_grad[...] = grad
    for c in outs:
        c.wait_send()


def combine(parts, probs, metas, routes):
    vmem = pl.BlockSpec(memory_space=pltpu.VMEM)
    anywhere = pl.BlockSpec(memory_space=pl.ANY)
    bf = jnp.bfloat16
    dma = pltpu.SemaphoreType.DMA
    seg = jnp.broadcast_to(jnp.asarray(SEG, jnp.float32)[:, :, None], (2, PLANE, 128))
    return pl.pallas_call(
        combine_kernel,
        out_shape=(
            jax.ShapeDtypeStruct((TOK, D), bf),
            jax.ShapeDtypeStruct((TOK, TOP), jnp.float32),
        ),
        in_specs=[anywhere, anywhere, vmem, vmem, vmem, vmem],
        out_specs=(vmem, vmem),
        scratch_shapes=[pltpu.VMEM((CLASS, D), bf), pltpu.VMEM((CLASS, D), bf)]
        + [pltpu.VMEM((CLASS, 128), jnp.float32) for _ in range(2)]
        + [pltpu.VMEM((CLASS, w), bf) for w in BACK_WIDE]
        + [pltpu.VMEM((CLASS, w), bf) for w in BACK_WIDE]
        + [pltpu.VMEM((PLANE, w // 2), bf) for w in BACK_WIDE]
        + [pltpu.VMEM((3, 192, w // 2), bf) for w in BACK_WIDE]
        + [pltpu.VMEM((192, w // 2), bf) for w in BACK_WIDE]
        + [pltpu.VMEM((3, BLOCK, w // 2), bf) for w in BACK_WIDE]
        + [dma((4,)), dma((4,)), dma((2,))]
        + [dma((3, 3)) for _ in range(6)],
        compiler_params=pltpu.CompilerParams(
            collective_id=2, has_side_effects=True, vmem_limit_bytes=56 * 2**20
        ),
        name="combine",
    )(
        parts, probs, metas, routes,
        jnp.asarray(PERM.transpose(0, 2, 1), jnp.bfloat16), seg,
    )


def on_device(tokens, out_grad, routes, gate_probs, gate_weight, up_weight, down_weight):
    rows_t, rows_g, picked, metas = dispatch(tokens, out_grad, routes, gate_probs)
    rows_in = rows_t.reshape(2 * CLASS, D)
    grads_in = rows_g.reshape(2 * CLASS, D)
    expert = lax.axis_index("dp") * 16 + lax.axis_index("expert") // 2
    lane = lax.broadcasted_iota(jnp.int32, (2 * CLASS, 128), 1)
    weight = jnp.sum(
        jnp.where(lane == 64 + expert, picked.reshape(2 * CLASS, 128).astype(jnp.float32), 0.0),
        axis=1, keepdims=True,
    )
    gate_half, up_half, down_half = gate_weight[0], up_weight[0], down_weight[0]
    gate_pre = jnp.dot(rows_in, gate_half, preferred_element_type=jnp.float32)
    up_pre = jnp.dot(rows_in, up_half, preferred_element_type=jnp.float32)
    sigmoid = jax.nn.sigmoid(gate_pre)
    active = gate_pre * sigmoid
    hidden = active * up_pre
    raw_grad = lax.dot_general(
        grads_in, down_half, (((1,), (1,)), ((), ())), preferred_element_type=jnp.float32
    )
    prob_part = jnp.sum(hidden * raw_grad, axis=1, keepdims=True).astype(jnp.bfloat16)
    scaled_grad = weight * raw_grad
    gate_delta = (scaled_grad * up_pre * sigmoid * (1.0 + gate_pre * (1.0 - sigmoid))).astype(
        jnp.bfloat16
    )
    up_delta = (scaled_grad * active).astype(jnp.bfloat16)
    scaled_hidden = (weight * hidden).astype(jnp.bfloat16)
    gate_sum = lax.dot_general(
        rows_in, gate_delta, (((0,), (0,)), ((), ())), preferred_element_type=jnp.float32
    )
    up_sum = lax.dot_general(
        rows_in, up_delta, (((0,), (0,)), ((), ())), preferred_element_type=jnp.float32
    )
    down_sum = lax.dot_general(
        scaled_hidden, grads_in, (((0,), (0,)), ((), ())), preferred_element_type=jnp.float32
    )
    input_part = (
        lax.dot_general(
            gate_delta, gate_half, (((1,), (1,)), ((), ())), preferred_element_type=jnp.float32
        )
        + lax.dot_general(
            up_delta, up_half, (((1,), (1,)), ((), ())), preferred_element_type=jnp.float32
        )
    ).astype(jnp.bfloat16)
    probs = jnp.broadcast_to(prob_part.astype(jnp.float32), (2 * CLASS, 128))
    token_grad, prob_grad = combine(
        input_part.reshape(2, CLASS, D), probs.reshape(2, CLASS, 128), metas, routes
    )
    return (
        token_grad,
        prob_grad,
        gate_sum.astype(jnp.bfloat16)[None],
        up_sum.astype(jnp.bfloat16)[None],
        down_sum.astype(jnp.bfloat16)[None],
    )


def solution(mesh):
    two, three = P(("dp", "expert"), None), P(("dp", "expert"), None, None)
    return jax.shard_map(
        on_device,
        mesh=mesh,
        in_specs=(two, two, two, two, three, three, three),
        out_specs=(two, two, three, three, three),
        check_vma=False,
    )
```

```python
import numpy as np
import jax
import jax.numpy as jnp
from jax import lax
from jax.sharding import PartitionSpec as P
from jax.experimental import pallas as pl
from jax.experimental.pallas import tpu as pltpu

MESH = pl.DeviceIdType.MESH
BF = jnp.bfloat16
F32 = jnp.float32
D = 4096
HALF = 384
TOK = 24
TOP = 8
CAP = 6
RING = 4
SLOTS = 16 * CAP
CLASS = RING * SLOTS
ROWS = 2 * CLASS
BLOCK = 2 * TOK
PLANE = 16 * BLOCK
LINE = 4 * BLOCK
STEP = 512
X, Y, Z = 0, 1, 2
ORDERS = ((Z, Y, X), (X, Z, Y), (Y, X, Z))
T_AT, T_HALF = (0, 1536, 2816), (768, 640, 640)
G_AT, G_HALF = (0, 1280, 2816), (640, 768, 640)
T_WIDE = (896, 768, 768)
T_SENT = (768, 640, 768)
BACK = (768, 640, 768)


def place_tables():
    i = np.arange(CLASS)
    x, y, z, r = i // 96, i // 24 % 4, i // 6 % 4, i % 6
    rows = (y * 96 + (z * 4 + x) * 6 + r, z * 96 + (x * 4 + y) * 6 + r)
    perm = np.stack([(np.arange(CLASS)[None, :] == w[:, None]) for w in rows]).astype(np.float32)
    k = np.arange(PLANE)
    seg = np.stack([k // BLOCK * CAP, k % BLOCK // TOK]).astype(np.float32)
    return perm, seg


PERM, SEG = place_tables()


def position():
    dp, ex = lax.axis_index("dp"), lax.axis_index("expert")
    return (lax.rem(ex // 2, 4), ex // 8, dp), lax.rem(ex, 2)


def device(co, core):
    return (co[2], co[1] * 8 + co[0] * 2 + core)


def shifted(co, axis, by):
    out = list(co)
    out[axis] = lax.rem(co[axis] + by, RING)
    return tuple(out)


def enter(co, core):
    barrier = pltpu.get_barrier_semaphore()
    for axis in (X, Y, Z):
        for by in (1, 2, 3):
            pl.semaphore_signal(
                barrier, inc=1, device_id=device(shifted(co, axis, by), core), device_id_type=MESH
            )
    pl.semaphore_signal(barrier, inc=1, device_id=device(co, 1 - core), device_id_type=MESH)
    pl.semaphore_wait(barrier, 10)


def remote(src, dst, send, recv, to):
    return pltpu.make_async_remote_copy(
        src_ref=src, dst_ref=dst, send_sem=send, recv_sem=recv, device_id=to, device_id_type=MESH
    )


def expert_of(co):
    return co[2] * 16 + co[1] * 4 + co[0]


def rows_at(start, size):
    return pl.ds(pl.multiple_of(start, 16), size)


def dot(a, b, over=((1,), (0,))):
    return lax.dot_general(a, b, (over, ((), ())), preferred_element_type=F32)


def routing_tile(routes, probs):
    lane = lax.broadcasted_iota(jnp.int32, (TOK, 128), 1)
    named = jnp.zeros((TOK, 128), F32)
    weight = jnp.zeros((TOK, 128), F32)
    for k in range(TOP):
        route = routes[:, k:k + 1]
        named = named + jnp.where(lane == route, 1.0, 0.0)
        weight = weight + jnp.where(lane == route + 64, probs[:, k:k + 1].astype(F32), 0.0)
    before = lax.broadcasted_iota(jnp.int32, (TOK, TOK), 0) > lax.broadcasted_iota(
        jnp.int32, (TOK, TOK), 1
    )
    rank = dot(jnp.where(before, 1.0, 0.0), named)
    meta = named * (rank + 1.0) + weight
    return jnp.concatenate([meta, meta], axis=0).astype(BF)


def kernel(
    tok, grd, routes, probs, perm, perm_t, seg_row, seg_col, gate_w, up_w, down_w,
    token_grad, prob_grad, gate_out, up_out, down_out,
    rows_t, rows_g, wgu, wd,
    gt0, gt1, gt2, gg0, gg1, gg2, st0, st1, st2, sg0, sg1, sg2, rt0, rt1, rt2, rg0, rg1, rg2,
    pk, meta2, other0, other1, other2, rr0, rr1, rr2, bs0, bs1, bs2, us0, us1, us2, cs0, cs1, cs2,
    gu, delta, hid, pp, stage_gu, stage_d,
    a1_s, a1_r, a2_s, a2_r, x_s, x_r, d_s, d_r, m_s, m_r, h_s, h_r,
    y_s, y_r, b2_s, b2_r, b1_s, b1_r, l_s, o_s,
):
    co, core = position()
    partner = device(co, 1 - core)
    gts, ggs = (gt0, gt1, gt2), (gg0, gg1, gg2)
    gat = (gts, ggs)
    sel = ((st0, st1, st2), (sg0, sg1, sg2))
    rec = ((rt0, rt1, rt2), (rg0, rg1, rg2))
    others, rrs, bss = (other0, other1, other2), (rr0, rr1, rr2), (bs0, bs1, bs2)
    uss, css = (us0, us1, us2), (cs0, cs1, cs2)
    at_of, half_of = (T_AT, G_AT), (T_HALF, G_HALF)
    gat_wide = (T_WIDE, G_HALF)
    sent = (T_SENT, G_HALF)
    outs = []

    def send(src, dst, s, r, to):
        c = remote(src, dst, s, r, to)
        c.start()
        outs.append(c)

    def arrive(ref, s, r):
        remote(ref, ref, s, r, partner).wait_recv()

    loads = [
        pltpu.make_async_copy(gate_w.at[0], wgu.at[:, 0:HALF], l_s.at[0]),
        pltpu.make_async_copy(up_w.at[0], wgu.at[:, HALF:2 * HALF], l_s.at[1]),
        pltpu.make_async_copy(down_w.at[0], wd, l_s.at[2]),
    ]
    for c in loads:
        c.start()
    meta = routing_tile(routes, probs)
    enter(co, core)

    def own_slot(p):
        a1, a2, a3 = ORDERS[p]
        return rows_at((co[a2] * 4 + co[a1]) * BLOCK, BLOCK)

    for q, src in enumerate((tok, grd)):
        for p, (a1, a2, a3) in enumerate(ORDERS):
            at, h = at_of[q][p], half_of[q][p]
            both = jnp.concatenate(
                [src[:, at:at + h].astype(F32), src[:, at + h:at + 2 * h].astype(F32)], axis=0
            )
            ref = gat[q][p]
            ref[own_slot(p), 0:h] = both.astype(BF)
            if q == 0:
                ref[own_slot(p), h:h + 128] = meta
            wide = gat_wide[q][p]
            for by in (1, 3, 2):
                view = ref.at[own_slot(p), 0:wide]
                send(
                    view, view, a1_s.at[q, p, by - 1], a1_r.at[q, p, by - 1],
                    device(shifted(co, a1, by), core),
                )

    def part_of_line(q, p, b, which):
        return gat[q][p].at[rows_at(b * LINE + which * (LINE // 2), LINE // 2), 0:gat_wide[q][p]]

    def second_own(q):
        for p, (a1, a2, a3) in enumerate(ORDERS):
            for by in (1, 3, 2):
                theirs = rows_at((co[a2] * 4 + lax.rem(co[a1] + 4 - by, 4)) * BLOCK, BLOCK)
                arrive(
                    gat[q][p].at[theirs, 0:gat_wide[q][p]],
                    a1_s.at[q, p, by - 1], a1_r.at[q, p, by - 1],
                )
            up, down = device(shifted(co, a2, 1), core), device(shifted(co, a2, 3), core)
            for idx, which, to in ((0, 0, up), (3, 1, down), (1, 1, up), (4, 0, down)):
                ref = part_of_line(q, p, co[a2], which)
                send(ref, ref, a2_s.at[q, p, idx], a2_r.at[q, p, idx], to)

    def second_pass(q):
        for p, (a1, a2, a3) in enumerate(ORDERS):
            up, down = device(shifted(co, a2, 1), core), device(shifted(co, a2, 3), core)
            for got, idx, by, which, to in ((0, 2, 3, 0, up), (3, 5, 1, 1, down)):
                ref = part_of_line(q, p, lax.rem(co[a2] + by, 4), which)
                arrive(ref, a2_s.at[q, p, got], a2_r.at[q, p, got])
                send(ref, ref, a2_s.at[q, p, idx], a2_r.at[q, p, idx], to)

    def second_wait(q, p):
        a1, a2, a3 = ORDERS[p]
        for idx, by, which in ((1, 3, 1), (4, 1, 0), (2, 2, 0), (5, 2, 1)):
            arrive(
                part_of_line(q, p, lax.rem(co[a2] + by, 4), which),
                a2_s.at[q, p, idx], a2_r.at[q, p, idx],
            )

    def wanted(p):
        a1, a2, a3 = ORDERS[p]
        h = T_HALF[p]
        line = lax.broadcasted_iota(jnp.int32, (8, 128), 0)
        lane = lax.broadcasted_iota(jnp.int32, (8, 128), 1)
        name = jnp.full((8, 128), -1, jnp.int32)
        for by in range(4):
            name = jnp.where(line == by, expert_of(shifted(co, a3, by)), name)
        pick = jnp.where(lane == name, 1.0, 0.0).astype(BF)
        val = dot(pick, gts[p][:, h:h + 128], ((1,), (1,)))
        return jnp.where(val > 0.5, val - 1.0 + seg_row[0:1, :], -1.0)

    slot = lax.broadcasted_iota(jnp.int32, (SLOTS, PLANE), 0).astype(F32)
    top = seg_row[1:2, :] < 0.5

    def choose(q, p, want, by):
        a1, a2, a3 = ORDERS[p]
        row = want[by:by + 1, :]
        pick = jnp.concatenate(
            [
                jnp.where(slot == jnp.where(top, row, -1.0), 1.0, 0.0),
                jnp.where(slot == jnp.where(top, -1.0, row), 1.0, 0.0),
            ],
            axis=0,
        ).astype(BF)
        w = sent[q][p]
        got = dot(pick, gat[q][p][:, 0:w]).astype(BF)
        mine = rows_at(co[a3] * 192, 192)
        if by == 0:
            rec[q][p][mine, 0:w] = got
        else:
            sel[q][p][by - 1] = got
            send(
                sel[q][p].at[by - 1], rec[q][p].at[mine, 0:w],
                x_s.at[q, p, by - 1], x_r.at[q, p, by - 1], device(shifted(co, a3, by), core),
            )

    mine = rows_at(core * CLASS, CLASS)
    theirs = rows_at((1 - core) * CLASS, CLASS)

    def reorder(q, p, out):
        a1, a2, a3 = ORDERS[p]
        w = sent[q][p]
        for by in (1, 3, 2):
            ref = rec[q][p].at[rows_at(lax.rem(co[a3] + 4 - by, 4) * 192, 192), 0:w]
            arrive(ref, x_s.at[q, p, by - 1], x_r.at[q, p, by - 1])
        at, h = at_of[q][p], half_of[q][p]
        for n in range(2):
            full = jnp.concatenate(
                [rec[q][p][b * 192 + n * 96:b * 192 + n * 96 + 96, 0:w] for b in range(4)], axis=0
            )
            if p > 0:
                full = dot(perm[p - 1], full).astype(BF)
            out[mine, at + n * h:at + n * h + h] = full[:, 0:h]
            if q == 0 and p == 2 and n == 0:
                pk[mine, :] = full[:, h:h + 128]
                send(pk.at[mine], pk.at[mine], m_s.at[0], m_r.at[0], partner)
        view = out.at[mine, at:at + 2 * h]
        send(view, view, d_s.at[q, p], d_r.at[q, p], partner)

    def swapped(q, p, out):
        at, h = at_of[q][p], half_of[q][p]
        arrive(out.at[theirs, at:at + 2 * h], d_s.at[q, p], d_r.at[q, p])

    second_own(0)
    second_pass(0)
    second_own(1)
    wants = []
    for p in range(3):
        second_wait(0, p)
        wants.append(wanted(p))
        for by in (1, 3, 2, 0):
            choose(0, p, wants[p], by)
        if p == 0:
            second_pass(1)
    for p in range(3):
        second_wait(1, p)
        for by in (1, 3, 2, 0):
            choose(1, p, wants[p], by)
    meta2[...] = gts[2][:, 640:768]
    for p in range(3):
        reorder(0, p, rows_t)
    for c in loads:
        c.wait()
    gu[mine, :] = dot(rows_t[mine, :], wgu[...])
    for p in range(3):
        swapped(0, p, rows_t)
    arrive(pk.at[theirs], m_s.at[0], m_r.at[0])
    gu[theirs, :] = dot(rows_t[theirs, :], wgu[...])
    for p in range(3):
        reorder(1, p, rows_g)

    early = list(outs)
    outs.clear()

    def local_terms(rows):
        gate, up = gu[rows, 0:HALF], gu[rows, HALF:2 * HALF]
        raw = dot(rows_g[rows, :], wd[...], ((1,), (1,)))
        lane = lax.broadcasted_iota(jnp.int32, (CLASS, 128), 1)
        weight = jnp.sum(
            jnp.where(lane == 64 + expert_of(co), pk[rows, :].astype(F32), 0.0),
            axis=1, keepdims=True,
        )
        sig = jax.nn.sigmoid(gate)
        active = gate * sig
        hidden = active * up
        scaled = weight * raw
        delta[rows, 0:HALF] = (scaled * up * sig * (1.0 + gate * (1.0 - sig))).astype(BF)
        delta[rows, HALF:2 * HALF] = (scaled * active).astype(BF)
        hid[rows, :] = (weight * hidden).astype(BF)
        part = jnp.sum(hidden * raw, axis=1, keepdims=True)
        pp[rows, :] = jnp.where(lane == expert_of(co), part, 0.0).astype(BF)

    def input_part(rows, p, out):
        at, h = T_AT[p], T_HALF[p]
        d, tile = delta[rows, :], pp[rows, :]
        if p > 0:
            d = dot(perm_t[p - 1], d).astype(BF)
            if p == 2:
                tile = dot(perm_t[p - 1], tile).astype(BF)
        for n in range(2):
            val = dot(d, wgu[at + n * h:at + n * h + h, :], ((1,), (1,))).astype(BF)
            if p == 2:
                val = jnp.concatenate([val, tile if n == 0 else jnp.zeros_like(tile)], axis=1)
            for b in range(4):
                out[b * 192 + n * 96:b * 192 + n * 96 + 96, 0:BACK[p]] = val[b * 96:b * 96 + 96, :]

    local_terms(mine)
    for p in range(3):
        swapped(1, p, rows_g)
    local_terms(theirs)
    away = (rg1, rg0, rg2)
    for p in range(3):
        w = BACK[p]
        input_part(theirs, p, away[p])
        send(away[p].at[:, 0:w], others[p], h_s.at[p], h_r.at[p], partner)
    for p, (a1, a2, a3) in enumerate(ORDERS):
        input_part(mine, p, rec[0][p])
        arrive(others[p], h_s.at[p], h_r.at[p])
        ref = rec[0][p]
        total = ref[...].astype(F32) + others[p][...].astype(F32)
        if p < 2:
            ref[...] = total.astype(BF)
        else:
            ref[:, 0:640] = total[:, 0:640].astype(BF)
            for b in range(4):
                tile = total[b * 192:b * 192 + 96, 640:768]
                hi = tile.astype(BF)
                ref[b * 192:b * 192 + 96, 640:768] = hi
                ref[b * 192 + 96:b * 192 + 192, 640:768] = (tile - hi.astype(F32)).astype(BF)
        for by in (1, 3, 2):
            to = shifted(co, a3, by)
            send(
                ref.at[rows_at(to[a3] * 192, 192)], rrs[p].at[rows_at(co[a3] * 192, 192)],
                y_s.at[p, by - 1], y_r.at[p, by - 1], device(to, core),
            )
        rrs[p][rows_at(co[a3] * 192, 192), :] = ref[rows_at(co[a3] * 192, 192), :]

    def down_step(i, carry):
        for n in range(2):
            @pl.when(i > 0)
            def _():
                pltpu.make_async_copy(
                    stage_d.at[n], down_out.at[0, :, 0:STEP], o_s.at[n]
                ).wait()
            cols = pl.ds(pl.multiple_of((2 * i + n) * STEP, STEP), STEP)
            stage_d[n] = dot(hid[...], rows_g[:, cols], ((0,), (0,))).astype(BF)
            pltpu.make_async_copy(stage_d.at[n], down_out.at[0, :, cols], o_s.at[n]).start()
        return carry

    def gate_up_step(i, carry):
        for n in range(2):
            @pl.when(i > 0)
            def _():
                for m, out in enumerate((gate_out, up_out)):
                    pltpu.make_async_copy(
                        stage_gu.at[n, :, m * HALF:m * HALF + HALF], out.at[0, 0:STEP, :],
                        o_s.at[2 + 2 * n + m],
                    ).wait()
            cols = pl.ds(pl.multiple_of((2 * i + n) * STEP, STEP), STEP)
            stage_gu[n] = dot(rows_t[:, cols], delta[...], ((0,), (0,))).astype(BF)
            for m, out in enumerate((gate_out, up_out)):
                pltpu.make_async_copy(
                    stage_gu.at[n, :, m * HALF:m * HALF + HALF], out.at[0, cols, :],
                    o_s.at[2 + 2 * n + m],
                ).start()
        return carry

    lax.fori_loop(0, 4, down_step, 0)

    for c in early:
        c.wait_send()
    code = lax.broadcasted_iota(jnp.int32, (PLANE, PLANE), 1).astype(F32)
    sums = gts
    for p, (a1, a2, a3) in enumerate(ORDERS):
        w = BACK[p]
        line = lax.broadcasted_iota(jnp.int32, (128, 128), 0)
        lane = lax.broadcasted_iota(jnp.int32, (128, 128), 1)
        name = jnp.full((128, 128), -1, jnp.int32)
        for b in range(4):
            at_b = list(co)
            at_b[a3] = b
            name = jnp.where(line == b, expert_of(at_b), name)
        pick = jnp.where(lane == name, 1.0, 0.0).astype(BF)
        tile = meta2[...] if p == 2 else gts[p][:, T_HALF[p]:T_HALF[p] + 128]
        val = dot(tile, pick, ((1,), (1,)))
        lane = lax.broadcasted_iota(jnp.int32, (PLANE, 128), 1).astype(F32)
        spot = jnp.where(
            val > 0.5, val - 1.0 + seg_col[0] + lane * 192.0 + seg_col[1] * 96.0, -1.0
        )
        put = jnp.zeros((PLANE, PLANE), F32)
        for b in range(4):
            put = jnp.where(code == spot[:, b:b + 1], 1.0, put)
        put = put.astype(BF)
        for by in (1, 3, 2):
            ref = rrs[p].at[rows_at(lax.rem(co[a3] + 4 - by, 4) * 192, 192)]
            arrive(ref, y_s.at[p, by - 1], y_r.at[p, by - 1])
        sums[p][:, 0:w] = dot(put, rrs[p][...]).astype(BF)
        for by in (1, 3, 2):
            to = shifted(co, a2, by)
            send(
                sums[p].at[rows_at(to[a2] * LINE, LINE), 0:w], bss[p].at[by - 1],
                b2_s.at[p, by - 1], b2_r.at[p, by - 1], device(to, core),
            )
    lax.fori_loop(0, 4, gate_up_step, 0)
    for p, (a1, a2, a3) in enumerate(ORDERS):
        total = sums[p][rows_at(co[a2] * LINE, LINE), 0:BACK[p]].astype(F32)
        for by in (1, 3, 2):
            arrive(bss[p].at[by - 1], b2_s.at[p, by - 1], b2_r.at[p, by - 1])
            total = total + bss[p][by - 1].astype(F32)
        uss[p][...] = total.astype(BF)
        for by in (1, 3, 2):
            to = shifted(co, a1, by)
            send(
                uss[p].at[rows_at(to[a1] * BLOCK, BLOCK)], css[p].at[by - 1],
                b1_s.at[p, by - 1], b1_r.at[p, by - 1], device(to, core),
            )
    for p, (a1, a2, a3) in enumerate(ORDERS):
        total = uss[p][rows_at(co[a1] * BLOCK, BLOCK), :].astype(F32)
        for by in (1, 3, 2):
            arrive(css[p].at[by - 1], b1_s.at[p, by - 1], b1_r.at[p, by - 1])
            total = total + css[p][by - 1].astype(F32)
        at, h = T_AT[p], T_HALF[p]
        token_grad[:, at:at + h] = total[0:TOK, 0:h].astype(BF)
        token_grad[:, at + h:at + 2 * h] = total[TOK:, 0:h].astype(BF)
        if p == 2:
            per = total[0:TOK, h:h + 128] + total[TOK:, h:h + 128]
            lane = lax.broadcasted_iota(jnp.int32, (TOK, 128), 1)
            spot = lax.broadcasted_iota(jnp.int32, (TOK, TOP), 1)
            grad = jnp.zeros((TOK, TOP), F32)
            for k in range(TOP):
                one = jnp.sum(jnp.where(lane == routes[:, k:k + 1], per, 0.0), axis=1, keepdims=True)
                grad = jnp.where(spot == k, one, grad)
            prob_grad[...] = grad
    for n in range(2):
        pltpu.make_async_copy(stage_d.at[n], down_out.at[0, :, 0:STEP], o_s.at[n]).wait()
        for m, out in enumerate((gate_out, up_out)):
            pltpu.make_async_copy(
                stage_gu.at[n, :, m * HALF:m * HALF + HALF], out.at[0, 0:STEP, :],
                o_s.at[2 + 2 * n + m],
            ).wait()
    for c in outs:
        c.wait_send()


def on_device(tokens, out_grad, routes, gate_probs, gate_weight, up_weight, down_weight):
    vmem = pl.BlockSpec(memory_space=pltpu.VMEM)
    anywhere = pl.BlockSpec(memory_space=pl.ANY)
    dma = pltpu.SemaphoreType.DMA
    seg = jnp.asarray(SEG, F32)
    shapes = [(ROWS, D), (ROWS, D), (D, 2 * HALF), (HALF, D)]
    shapes += [(PLANE, 896), (PLANE, 768), (PLANE, 768)] + [(PLANE, w) for w in G_HALF]
    shapes += [(3, 192, w) for w in T_SENT] + [(3, 192, w) for w in G_HALF]
    shapes += [(ROWS, w) for w in T_SENT] + [(ROWS, w) for w in (640, 768, 768)]
    shapes += [(ROWS, 128), (PLANE, 128)]
    shapes += [(ROWS, w) for w in BACK] * 2
    shapes += [(3, LINE, w) for w in BACK] + [(LINE, w) for w in BACK]
    shapes += [(3, BLOCK, w) for w in BACK]
    scratch = [pltpu.VMEM(s, BF) for s in shapes]
    scratch += [
        pltpu.VMEM((ROWS, 2 * HALF), F32), pltpu.VMEM((ROWS, 2 * HALF), BF),
        pltpu.VMEM((ROWS, HALF), BF), pltpu.VMEM((ROWS, 128), BF),
        pltpu.VMEM((2, STEP, 2 * HALF), BF), pltpu.VMEM((2, HALF, STEP), BF),
    ]
    for s in ((2, 3, 3), (2, 3, 6), (2, 3, 3), (2, 3), (1,), (3,), (3, 3), (3, 3), (3, 3)):
        scratch += [dma(s), dma(s)]
    scratch += [dma((3,)), dma((6,))]
    return pl.pallas_call(
        kernel,
        out_shape=(
            jax.ShapeDtypeStruct((TOK, D), BF),
            jax.ShapeDtypeStruct((TOK, TOP), F32),
            jax.ShapeDtypeStruct((1, D, HALF), BF),
            jax.ShapeDtypeStruct((1, D, HALF), BF),
            jax.ShapeDtypeStruct((1, HALF, D), BF),
        ),
        in_specs=[vmem] * 8 + [anywhere] * 3,
        out_specs=(vmem, vmem, anywhere, anywhere, anywhere),
        scratch_shapes=scratch,
        compiler_params=pltpu.CompilerParams(
            collective_id=1, has_side_effects=True, vmem_limit_bytes=63 * 2**20
        ),
        name="routed_backward",
    )(
        tokens, out_grad, routes, gate_probs,
        jnp.asarray(PERM, BF), jnp.asarray(PERM.transpose(0, 2, 1), BF),
        seg, jnp.broadcast_to(seg[:, :, None], (2, PLANE, 128)),
        gate_weight, up_weight, down_weight,
    )


def solution(mesh):
    two, three = P(("dp", "expert"), None), P(("dp", "expert"), None, None)
    return jax.shard_map(
        on_device,
        mesh=mesh,
        in_specs=(two, two, two, two, three, three, three),
        out_specs=(two, two, three, three, three),
        check_vma=False,
    )
```

```python
import numpy as np
import jax
import jax.numpy as jnp
from jax import lax
from jax.sharding import PartitionSpec as P
from jax.experimental import pallas as pl
from jax.experimental.pallas import tpu as pltpu

MESH = pl.DeviceIdType.MESH
BF = jnp.bfloat16
F32 = jnp.float32
D = 4096
HALF = 384
TOK = 24
TOP = 8
CAP = 6
RING = 4
SLOTS = 16 * CAP
CLASS = RING * SLOTS
ROWS = 2 * CLASS
BLOCK = 2 * TOK
PLANE = 16 * BLOCK
LINE = 4 * BLOCK
STEP = 256
X, Y, Z = 0, 1, 2
ORDERS = ((Z, Y, X), (X, Z, Y), (Y, X, Z))
T_AT, T_HALF = (0, 1536, 2816), (768, 640, 640)
G_AT, G_HALF = (0, 1280, 2816), (640, 768, 640)
T_WIDE = (896, 768, 768)
T_SENT = (768, 640, 768)
BACK = (768, 640, 768)
CUT = 384


def place_tables():
    i = np.arange(CLASS)
    x, y, z, r = i // 96, i // 24 % 4, i // 6 % 4, i % 6
    rows = (y * 96 + (z * 4 + x) * 6 + r, z * 96 + (x * 4 + y) * 6 + r)
    perm = np.stack([(np.arange(CLASS)[None, :] == w[:, None]) for w in rows]).astype(np.float32)
    return perm


PERM = place_tables()


def position():
    dp, ex = lax.axis_index("dp"), lax.axis_index("expert")
    return (lax.rem(ex // 2, 4), ex // 8, dp), lax.rem(ex, 2)


def device(co, core):
    return (co[2], co[1] * 8 + co[0] * 2 + core)


def shifted(co, axis, by):
    out = list(co)
    out[axis] = lax.rem(co[axis] + by, RING)
    return tuple(out)


def enter(co, core):
    barrier = pltpu.get_barrier_semaphore()
    for axis in (X, Y, Z):
        for by in (1, 2, 3):
            pl.semaphore_signal(
                barrier, inc=1, device_id=device(shifted(co, axis, by), core), device_id_type=MESH
            )
    pl.semaphore_signal(barrier, inc=1, device_id=device(co, 1 - core), device_id_type=MESH)
    pl.semaphore_wait(barrier, 10)


def remote(src, dst, send, recv, to):
    return pltpu.make_async_remote_copy(
        src_ref=src, dst_ref=dst, send_sem=send, recv_sem=recv, device_id=to, device_id_type=MESH
    )


def expert_of(co):
    return co[2] * 16 + co[1] * 4 + co[0]


def rows_at(start, size):
    return pl.ds(pl.multiple_of(start, 16), size)


def dot(a, b, over=((1,), (0,))):
    return lax.dot_general(a, b, (over, ((), ())), preferred_element_type=F32)


def segment(k):
    place = jnp.floor((k + 0.5) * (1.0 / BLOCK))
    half = jnp.where(k - place * BLOCK > TOK - 0.5, 1.0, 0.0)
    return place * CAP, half


def unit(n, dtype):
    return jnp.where(
        lax.broadcasted_iota(jnp.int32, (n, n), 0) == lax.broadcasted_iota(jnp.int32, (n, n), 1),
        1.0, 0.0,
    ).astype(dtype)


def routing_tile(routes, probs):
    lane = lax.broadcasted_iota(jnp.int32, (TOK, 128), 1).astype(F32)
    named = jnp.zeros((TOK, 128), F32)
    weight = jnp.zeros((TOK, 128), F32)
    for k in range(TOP):
        route = routes[:, k:k + 1]
        named = named + jnp.where(lane == route, 1.0, 0.0)
        weight = weight + jnp.where(lane == route + 64.0, probs[:, k:k + 1], 0.0)
    before = lax.broadcasted_iota(jnp.int32, (TOK, TOK), 0) > lax.broadcasted_iota(
        jnp.int32, (TOK, TOK), 1
    )
    rank = dot(jnp.where(before, 1.0, 0.0), named)
    meta = named * (rank + 1.0) + weight
    return jnp.concatenate([meta, meta], axis=0).astype(BF)


def kernel(
    tok, grd, routes_in, probs_in, perm_in, gate_w, up_w, down_w,
    token_grad, prob_grad, gate_out, up_out, down_out,
    rows_t, rows_g, wgu, wd,
    gt0, gt1, gt2, gg0, gg1, gg2, st0, st1, st2, sg0, sg1, sg2, rt0, rt1, rt2, rg0, rg1, rg2,
    rr0, rr1, rr2, bs0, bs1, bs2, cs0, cs1, cs2,
    perm, delta, hid, gu,
    a1_s, a1_r, a2_s, a2_r, x_s, x_r, d_s, d_r, w_s, w_r, h_s, h_r,
    y_s, y_r, b2_s, b2_r, b1_s, b1_r, l_s, o_s,
):
    co, core = position()
    partner = device(co, 1 - core)
    gts, ggs = (gt0, gt1, gt2), (gg0, gg1, gg2)
    gat = (gts, ggs)
    sel = ((st0, st1, st2), (sg0, sg1, sg2))
    rec = ((rt0, rt1, rt2), (rg0, rg1, rg2))
    rrs, bss = (rr0, rr1, rr2), (bs0, bs1, bs2)
    css = (cs0, cs1, cs2)
    delta_o, hid_o, ptile = st0.at[0:CLASS], st2.at[0:CLASS, 0:HALF], st1.at[0:CLASS, 0:256]
    pk = gt0.at[0:CLASS, 768:896]
    uss = (st0.at[CLASS:576], st1.at[CLASS:576], st2.at[CLASS:576])
    at_of, half_of = (T_AT, G_AT), (T_HALF, G_HALF)
    gat_wide = (T_WIDE, G_HALF)
    sent = (T_SENT, G_HALF)
    outs = []

    def send(src, dst, s, r, to):
        c = remote(src, dst, s, r, to)
        c.start()
        outs.append(c)

    def arrive(ref, s, r):
        remote(ref, ref, s, r, partner).wait_recv()

    def settle():
        for c in outs:
            c.wait_send()
        outs.clear()

    H2 = 2 * HALF
    loads = [
        pltpu.make_async_copy(gate_w.at[0], wgu.at[:, 0:HALF], l_s.at[0]),
        pltpu.make_async_copy(up_w.at[0], wgu.at[:, HALF:H2], l_s.at[1]),
        pltpu.make_async_copy(down_w.at[0], wd.at[0:HALF], l_s.at[2]),
        pltpu.make_async_copy(perm_in, perm, l_s.at[3]),
    ]
    for c in loads:
        c.start()
    eye = unit(TOK, F32)
    routes = dot(eye, routes_in[...].astype(F32), ((1,), (1,)))
    meta = routing_tile(routes, dot(eye, probs_in[...].astype(F32), ((1,), (1,))))

    def own_slot(p):
        a1, a2, a3 = ORDERS[p]
        return rows_at((co[a2] * 4 + co[a1]) * BLOCK, BLOCK)

    def pack(q, src):
        for p in range(3):
            at, h = at_of[q][p], half_of[q][p]
            both = jnp.concatenate(
                [src[:, at:at + h].astype(F32), src[:, at + h:at + 2 * h].astype(F32)], axis=0
            )
            gat[q][p][own_slot(p), 0:h] = both.astype(BF)
            if q == 0:
                gat[q][p][own_slot(p), h:h + 128] = meta

    def first(q):
        for p, (a1, a2, a3) in enumerate(ORDERS):
            view = gat[q][p].at[own_slot(p), 0:gat_wide[q][p]]
            for by in (1, 3, 2):
                send(
                    view, view, a1_s.at[q, p, by - 1], a1_r.at[q, p, by - 1],
                    device(shifted(co, a1, by), core),
                )

    pack(0, tok)
    enter(co, core)
    first(0)
    pack(1, grd)
    first(1)
    gathered = list(outs)
    outs.clear()
    send(gate_w.at[0], wgu.at[:, H2:H2 + HALF], w_s.at[0], w_r.at[0], partner)
    send(up_w.at[0], wgu.at[:, H2 + HALF:2 * H2], w_s.at[1], w_r.at[1], partner)
    send(down_w.at[0], wd.at[HALF:H2], w_s.at[2], w_r.at[2], partner)
    weights = list(outs)
    outs.clear()

    def part_of_line(q, p, b, which):
        return gat[q][p].at[rows_at(b * LINE + which * (LINE // 2), LINE // 2), 0:gat_wide[q][p]]

    def second_own(q):
        for p, (a1, a2, a3) in enumerate(ORDERS):
            for by in (1, 3, 2):
                theirs = rows_at((co[a2] * 4 + lax.rem(co[a1] + 4 - by, 4)) * BLOCK, BLOCK)
                arrive(
                    gat[q][p].at[theirs, 0:gat_wide[q][p]],
                    a1_s.at[q, p, by - 1], a1_r.at[q, p, by - 1],
                )
            up, down = device(shifted(co, a2, 1), core), device(shifted(co, a2, 3), core)
            for idx, which, to in ((0, 0, up), (3, 1, down), (1, 1, up), (4, 0, down)):
                ref = part_of_line(q, p, co[a2], which)
                send(ref, ref, a2_s.at[q, p, idx], a2_r.at[q, p, idx], to)
                gathered.append(outs.pop())

    def second_pass(q):
        for p, (a1, a2, a3) in enumerate(ORDERS):
            up, down = device(shifted(co, a2, 1), core), device(shifted(co, a2, 3), core)
            for got, idx, by, which, to in ((0, 2, 3, 0, up), (3, 5, 1, 1, down)):
                ref = part_of_line(q, p, lax.rem(co[a2] + by, 4), which)
                arrive(ref, a2_s.at[q, p, got], a2_r.at[q, p, got])
                send(ref, ref, a2_s.at[q, p, idx], a2_r.at[q, p, idx], to)
                gathered.append(outs.pop())

    def second_wait(q, p):
        a1, a2, a3 = ORDERS[p]
        for idx, by, which in ((1, 3, 1), (4, 1, 0), (2, 2, 0), (5, 2, 1)):
            arrive(
                part_of_line(q, p, lax.rem(co[a2] + by, 4), which),
                a2_s.at[q, p, idx], a2_r.at[q, p, idx],
            )

    k_row = lax.broadcasted_iota(jnp.int32, (1, PLANE), 1).astype(F32)
    place_row, half_row = segment(k_row)
    top = half_row < 0.5
    slot = lax.broadcasted_iota(jnp.int32, (SLOTS, PLANE), 0).astype(F32)

    def wanted(p):
        a1, a2, a3 = ORDERS[p]
        h = T_HALF[p]
        line = lax.broadcasted_iota(jnp.int32, (8, 128), 0)
        lane = lax.broadcasted_iota(jnp.int32, (8, 128), 1)
        name = jnp.full((8, 128), -1, jnp.int32)
        for by in range(4):
            name = jnp.where(line == by, expert_of(shifted(co, a3, by)), name)
        pick = jnp.where(lane == name, 1.0, 0.0).astype(BF)
        val = dot(pick, gts[p][:, h:h + 128], ((1,), (1,)))
        return jnp.where(val > 0.5, val - 1.0 + place_row, -1.0)

    def choose(q, p, want):
        a1, a2, a3 = ORDERS[p]
        picks = []
        for by in (1, 3, 2, 0):
            row = want[by:by + 1, :]
            picks.append(jnp.where(slot == jnp.where(top, row, -1.0), 1.0, 0.0).astype(BF))
            picks.append(jnp.where(slot == jnp.where(top, -1.0, row), 1.0, 0.0).astype(BF))
        w = sent[q][p]
        got = dot(jnp.concatenate(picks, axis=0), gat[q][p][:, 0:w]).astype(BF)
        mine = rows_at(co[a3] * 192, 192)
        for n, by in enumerate((1, 3, 2)):
            rows = slice(n * 192, n * 192 + 192)
            sel[q][p][rows, :] = got[rows]
            send(
                sel[q][p].at[rows], rec[q][p].at[mine, 0:w],
                x_s.at[q, p, by - 1], x_r.at[q, p, by - 1], device(shifted(co, a3, by), core),
            )
        rec[q][p][mine, 0:w] = got[576:768]

    def reorder(q, p, out):
        a1, a2, a3 = ORDERS[p]
        w = sent[q][p]
        for by in (1, 3, 2):
            ref = rec[q][p].at[rows_at(lax.rem(co[a3] + 4 - by, 4) * 192, 192), 0:w]
            arrive(ref, x_s.at[q, p, by - 1], x_r.at[q, p, by - 1])
        at, h = at_of[q][p], half_of[q][p]
        for n in range(2):
            full = jnp.concatenate(
                [rec[q][p][b * 192 + n * 96:b * 192 + n * 96 + 96, 0:w] for b in range(4)], axis=0
            )
            if p > 0:
                full = dot(perm[p - 1], full).astype(BF)
            out[0:CLASS, at + n * h:at + n * h + h] = full[:, 0:h]
            if q == 0 and p == 2 and n == 0:
                pk[...] = full[:, h:h + 128]
        send(
            out.at[0:CLASS, at:at + 2 * h], out.at[CLASS:ROWS, at:at + 2 * h],
            d_s.at[q, p], d_r.at[q, p], partner,
        )

    second_own(0)
    second_pass(0)
    second_own(1)
    wants = []
    for p in range(3):
        second_wait(0, p)
        wants.append(wanted(p))
        choose(0, p, wants[p])
        if p == 0:
            second_pass(1)
    for p in range(3):
        second_wait(1, p)
        choose(1, p, wants[p])
    for c in gathered:
        c.wait_send()
    exchanged = list(outs)
    outs.clear()
    code = lax.broadcasted_iota(jnp.int32, (LINE, PLANE), 1).astype(F32)
    k_col = lax.broadcasted_iota(jnp.int32, (PLANE, 128), 0).astype(F32)
    place_col, half_col = segment(k_col)
    for p, (a1, a2, a3) in enumerate(ORDERS):
        line = lax.broadcasted_iota(jnp.int32, (128, 128), 0)
        lane = lax.broadcasted_iota(jnp.int32, (128, 128), 1)
        name = jnp.full((128, 128), -1, jnp.int32)
        for b in range(4):
            at_b = list(co)
            at_b[a3] = b
            name = jnp.where(line == b, expert_of(at_b), name)
        pick = jnp.where(lane == name, 1.0, 0.0).astype(BF)
        val = dot(gts[p][:, T_HALF[p]:T_HALF[p] + 128], pick, ((1,), (1,)))
        lane = lax.broadcasted_iota(jnp.int32, (PLANE, 128), 1).astype(F32)
        spot = jnp.where(
            val > 0.5, val - 1.0 + place_col + lane * 192.0 + half_col * 96.0, -1.0
        )
        for r in range(0, PLANE, LINE):
            put = jnp.zeros((LINE, PLANE), F32)
            for b in range(4):
                put = jnp.where(code == spot[r:r + LINE, b:b + 1], 1.0, put)
            ggs[p][r:r + LINE, :] = put.astype(BF)
    for c in loads:
        c.wait()
    for p in range(3):
        reorder(0, p, rows_t)
    gu[:, 0:H2] = dot(rows_t[0:CLASS, :], wgu[:, 0:H2])
    arrive(wgu.at[:, H2:H2 + HALF], w_s.at[0], w_r.at[0])
    arrive(wgu.at[:, H2 + HALF:2 * H2], w_s.at[1], w_r.at[1])
    arrive(wd.at[HALF:H2], w_s.at[2], w_r.at[2])
    gu[:, H2:2 * H2] = dot(rows_t[0:CLASS, :], wgu[:, H2:2 * H2])
    for p in range(3):
        reorder(1, p, rows_g)

    for c in exchanged:
        c.wait_send()
    lane = lax.broadcasted_iota(jnp.int32, (CLASS, 128), 1)
    weight = jnp.sum(
        jnp.where(lane == 64 + expert_of(co), pk[...].astype(F32), 0.0), axis=1, keepdims=True
    )
    prob = jnp.zeros((CLASS, 1), F32)
    for n, (dl, hd) in enumerate(((delta, hid), (delta_o, hid_o))):
        gate, up = gu[:, n * H2:n * H2 + HALF], gu[:, n * H2 + HALF:n * H2 + H2]
        grad = dot(rows_g[0:CLASS, :], wd[n * HALF:n * HALF + HALF, :], ((1,), (1,)))
        sig = jax.nn.sigmoid(gate)
        active = gate * sig
        hidden = active * up
        scaled = weight * grad
        dl[0:CLASS, 0:HALF] = (scaled * up * sig * (1.0 + gate * (1.0 - sig))).astype(BF)
        dl[0:CLASS, HALF:H2] = (scaled * active).astype(BF)
        hd[0:CLASS, :] = (weight * hidden).astype(BF)
        prob = prob + jnp.sum(hidden * grad, axis=1, keepdims=True).astype(BF).astype(F32)
    prob = jnp.where(lane == expert_of(co), prob, 0.0)
    prob_hi = prob.astype(BF)
    ptile[:, 0:128] = prob_hi
    ptile[:, 128:256] = (prob - prob_hi.astype(F32)).astype(BF)

    def piece(p, c):
        h = CUT if c == 0 else T_HALF[p] - CUT
        return T_AT[p] + c * 2 * CUT, h, slice(c * CUT, c * CUT + h + (128 if (p, c) == (2, 1) else 0))

    def input_part(p, c):
        a1, a2, a3 = ORDERS[p]
        at, h, cols = piece(p, c)
        if p == 0:
            own, other = delta[0:CLASS, :], delta_o[...]
        else:
            if c == 0:
                rec[1][p][0:CLASS, :] = dot(perm[p - 1], delta[0:CLASS, :], ((0,), (0,))).astype(BF)
                rec[1][p][CLASS:ROWS, :] = dot(perm[p - 1], delta_o[...], ((0,), (0,))).astype(BF)
            own, other = rec[1][p][0:CLASS, :], rec[1][p][CLASS:ROWS, :]
        if (p, c) == (2, 1):
            tiles = dot(perm[p - 1], ptile[...], ((0,), (0,))).astype(BF)
        for n in range(2):
            w = slice(at + n * h, at + n * h + h)
            val = (
                dot(own, wgu[w, 0:H2], ((1,), (1,))) + dot(other, wgu[w, H2:2 * H2], ((1,), (1,)))
            ).astype(BF)
            if (p, c) == (2, 1):
                val = jnp.concatenate([val, tiles[:, n * 128:n * 128 + 128]], axis=1)
            for b in range(4):
                rec[0][p][b * 192 + n * 96:b * 192 + n * 96 + 96, cols] = val[b * 96:b * 96 + 96, :]
        for by in (1, 3, 2):
            to = shifted(co, a3, by)
            send(
                rec[0][p].at[rows_at(to[a3] * 192, 192), cols],
                rrs[p].at[rows_at(co[a3] * 192, 192), cols],
                y_s.at[c, p, by - 1], y_r.at[c, p, by - 1], device(to, core),
            )
        mine = rows_at(co[a3] * 192, 192)
        rrs[p][mine, cols] = rec[0][p][mine, cols]

    for c in range(2):
        for p in range(3):
            input_part(p, c)
    send(delta_o, delta.at[CLASS:ROWS], h_s.at[0], h_r.at[0], partner)
    send(hid_o, hid.at[CLASS:ROWS], h_s.at[1], h_r.at[1], partner)

    stage_d = (rg0.at[0:CLASS, 0:STEP], rg0.at[CLASS:ROWS, 0:STEP])
    stage_gu = (rg1, rg2)

    def down_out_copy(n, cols):
        return pltpu.make_async_copy(stage_d[n], down_out.at[0, :, cols], o_s.at[n])

    def gate_up_copies(n, cols):
        return [
            pltpu.make_async_copy(
                stage_gu[n].at[0:STEP, m * HALF:m * HALF + HALF], out.at[0, cols, :],
                o_s.at[2 + 2 * n + m],
            )
            for m, out in enumerate((gate_out, up_out))
        ]

    def down_step(i, carry):
        for n in range(2):
            @pl.when(i > 0)
            def _():
                down_out_copy(n, slice(0, STEP)).wait()
            cols = pl.ds(pl.multiple_of((2 * i + n) * STEP, STEP), STEP)
            stage_d[n][...] = dot(hid[...], rows_g[:, cols], ((0,), (0,))).astype(BF)
            down_out_copy(n, cols).start()
        return carry

    def gate_up_step(i, carry):
        for n in range(2):
            @pl.when(i > 0)
            def _():
                for c in gate_up_copies(n, slice(0, STEP)):
                    c.wait()
            cols = pl.ds(pl.multiple_of((2 * i + n) * STEP, STEP), STEP)
            stage_gu[n][0:STEP, :] = dot(rows_t[:, cols], delta[...], ((0,), (0,))).astype(BF)
            for c in gate_up_copies(n, cols):
                c.start()
        return carry

    sums = gts

    def relay(c):
        for p, (a1, a2, a3) in enumerate(ORDERS):
            cols = piece(p, c)[2]
            for by in (1, 3, 2):
                ref = rrs[p].at[rows_at(lax.rem(co[a3] + 4 - by, 4) * 192, 192), cols]
                arrive(ref, y_s.at[c, p, by - 1], y_r.at[c, p, by - 1])
            sums[p][:, cols] = dot(ggs[p][...], rrs[p][:, cols]).astype(BF)
            for by in (1, 3, 2):
                to = shifted(co, a2, by)
                send(
                    sums[p].at[rows_at(to[a2] * LINE, LINE), cols], bss[p].at[by - 1, :, cols],
                    b2_s.at[c, p, by - 1], b2_r.at[c, p, by - 1], device(to, core),
                )

    def line_sum(c):
        for p, (a1, a2, a3) in enumerate(ORDERS):
            cols = piece(p, c)[2]
            total = sums[p][rows_at(co[a2] * LINE, LINE), cols].astype(F32)
            for by in (1, 3, 2):
                arrive(bss[p].at[by - 1, :, cols], b2_s.at[c, p, by - 1], b2_r.at[c, p, by - 1])
                total = total + bss[p][by - 1, :, cols].astype(F32)
            uss[p][:, cols] = total.astype(BF)
            for by in (1, 3, 2):
                to = shifted(co, a1, by)
                send(
                    uss[p].at[rows_at(to[a1] * BLOCK, BLOCK), cols], css[p].at[by - 1, :, cols],
                    b1_s.at[c, p, by - 1], b1_r.at[c, p, by - 1], device(to, core),
                )

    def finish(c):
        for p, (a1, a2, a3) in enumerate(ORDERS):
            at, h, cols = piece(p, c)
            total = uss[p][rows_at(co[a1] * BLOCK, BLOCK), cols].astype(F32)
            for by in (1, 3, 2):
                arrive(css[p].at[by - 1, :, cols], b1_s.at[c, p, by - 1], b1_r.at[c, p, by - 1])
                total = total + css[p][by - 1, :, cols].astype(F32)
            token_grad[:, at:at + h] = total[0:TOK, 0:h].astype(BF)
            token_grad[:, at + h:at + 2 * h] = total[TOK:, 0:h].astype(BF)
            if (p, c) == (2, 1):
                per = total[0:TOK, h:h + 128] + total[TOK:, h:h + 128]
                lane = lax.broadcasted_iota(jnp.int32, (TOK, 128), 1).astype(F32)
                spot = lax.broadcasted_iota(jnp.int32, (TOK, TOP), 1)
                grad = jnp.zeros((TOK, TOP), F32)
                for k in range(TOP):
                    one = jnp.sum(
                        jnp.where(lane == routes[:, k:k + 1], per, 0.0), axis=1, keepdims=True
                    )
                    grad = jnp.where(spot == k, one, grad)
                prob_grad[...] = lax.dot_general(
                    unit(TOP, F32), grad, (((1,), (1,)), ((), ())),
                    preferred_element_type=F32, precision=lax.Precision.HIGHEST,
                )

    relay(0)
    for q, out in ((0, rows_t), (1, rows_g)):
        for p in range(3):
            at, h = at_of[q][p], half_of[q][p]
            arrive(out.at[CLASS:ROWS, at:at + 2 * h], d_s.at[q, p], d_r.at[q, p])
    arrive(delta.at[CLASS:ROWS], h_s.at[0], h_r.at[0])
    arrive(hid.at[CLASS:ROWS], h_s.at[1], h_r.at[1])
    lax.fori_loop(0, 8, down_step, 0)
    relay(1)
    line_sum(0)
    lax.fori_loop(0, 6, gate_up_step, 0)
    line_sum(1)
    lax.fori_loop(6, 8, gate_up_step, 0)
    finish(0)
    finish(1)
    for n in range(2):
        down_out_copy(n, slice(0, STEP)).wait()
        for c in gate_up_copies(n, slice(0, STEP)):
            c.wait()
    for c in weights:
        c.wait_send()
    settle()


def emit_kernel(token, prob, gate, up, down, token_out, prob_out, gate_out, up_out, down_out, held, held_d, sems):
    jobs = []
    for n, (src, dst) in enumerate(((gate, gate_out), (up, up_out), (down, down_out))):
        rows = src.shape[1] // 4
        for i in range(4):
            part = slice(i * rows, i * rows + rows)
            mid = held_d.at[part] if n == 2 else held.at[n, part]
            c = pltpu.make_async_copy(src.at[0, part], mid, sems.at[0, n, i])
            c.start()
            jobs.append((c, pltpu.make_async_copy(mid, dst.at[0, part], sems.at[1, n, i])))
    token_out[...] = token[...]
    prob_out[...] = prob[...]
    for c, d in jobs:
        c.wait()
        d.start()
    for c, d in jobs:
        d.wait()


def on_device(tokens, out_grad, routes, gate_probs, gate_weight, up_weight, down_weight):
    vmem = pl.BlockSpec(memory_space=pltpu.VMEM)
    anywhere = pl.BlockSpec(memory_space=pl.ANY)
    dma = pltpu.SemaphoreType.DMA
    shapes = [(ROWS, D), (ROWS, D), (D, 4 * HALF), (2 * HALF, D)]
    shapes += [(PLANE, 896), (PLANE, 768), (PLANE, 768)] + [(PLANE, 768)] * 3
    shapes += [(576, w) for w in T_SENT] + [(576, w) for w in G_HALF]
    shapes += [(ROWS, w) for w in T_SENT] + [(ROWS, w) for w in (640, 768, 768)]
    shapes += [(ROWS, w) for w in BACK]
    shapes += [(3, LINE, w) for w in BACK]
    shapes += [(3, BLOCK, w) for w in BACK]
    shapes += [PERM.shape, (ROWS, 2 * HALF), (ROWS, HALF)]
    scratch = [pltpu.VMEM(s, BF) for s in shapes] + [pltpu.VMEM((CLASS, 4 * HALF), F32)]
    for s in ((2, 3, 3), (2, 3, 6), (2, 3, 3), (2, 3), (3,), (2,)) + ((2, 3, 3),) * 3:
        scratch += [dma(s), dma(s)]
    scratch += [dma((4,)), dma((6,))]
    shaped = (
        jax.ShapeDtypeStruct((TOK, D), BF),
        jax.ShapeDtypeStruct((TOP, TOK), F32),
        jax.ShapeDtypeStruct((1, D, HALF), BF),
        jax.ShapeDtypeStruct((1, D, HALF), BF),
        jax.ShapeDtypeStruct((1, HALF, D), BF),
    )
    results = pl.pallas_call(
        kernel,
        out_shape=shaped,
        in_specs=[vmem] * 4 + [anywhere] * 4,
        out_specs=(vmem, vmem, anywhere, anywhere, anywhere),
        scratch_shapes=scratch,
        compiler_params=pltpu.CompilerParams(
            collective_id=1, has_side_effects=True, vmem_limit_bytes=65400 * 2**10
        ),
        name="routed_backward",
    )(
        tokens, out_grad, routes.T, gate_probs.T, jnp.asarray(PERM, BF),
        gate_weight, up_weight, down_weight,
    )
    token_grad, prob_grad, gate_grad, up_grad, down_grad = pl.pallas_call(
        emit_kernel,
        out_shape=shaped,
        in_specs=[vmem] * 2 + [anywhere] * 3,
        out_specs=(vmem, vmem, anywhere, anywhere, anywhere),
        scratch_shapes=[pltpu.VMEM((2, D, HALF), BF), pltpu.VMEM((HALF, D), BF), dma((2, 3, 4))],
        compiler_params=pltpu.CompilerParams(vmem_limit_bytes=62 * 2**20),
        name="emit",
    )(*results)
    return token_grad, prob_grad.T, gate_grad, up_grad, down_grad


def solution(mesh):
    two, three = P(("dp", "expert"), None), P(("dp", "expert"), None, None)
    return jax.shard_map(
        on_device,
        mesh=mesh,
        in_specs=(two, two, two, two, three, three, three),
        out_specs=(two, two, three, three, three),
        check_vma=False,
    )
```

```python
import numpy as np
import jax
import jax.numpy as jnp
from jax import lax
from jax.sharding import PartitionSpec as P
from jax.experimental import pallas as pl
from jax.experimental.pallas import tpu as pltpu

MESH = pl.DeviceIdType.MESH
BF = jnp.bfloat16
F32 = jnp.float32
D = 4096
HALF = 384
TOK = 24
TOP = 8
CAP = 6
RING = 4
SLOTS = 16 * CAP
CLASS = RING * SLOTS
ROWS = 2 * CLASS
BLOCK = 2 * TOK
PLANE = 16 * BLOCK
LINE = 4 * BLOCK
STEP = 512
X, Y, Z = 0, 1, 2
ORDERS = ((Z, Y, X), (X, Z, Y), (Y, X, Z))
T_AT, T_HALF = (0, 1536, 2816), (768, 640, 640)
G_AT, G_HALF = (0, 1280, 2816), (640, 768, 640)
T_WIDE = (896, 768, 768)
T_SENT = (768, 640, 768)
BACK = (768, 640, 768)
CUT = 384


def place_tables():
    i = np.arange(CLASS)
    x, y, z, r = i // 96, i // 24 % 4, i // 6 % 4, i % 6
    rows = (y * 96 + (z * 4 + x) * 6 + r, z * 96 + (x * 4 + y) * 6 + r)
    perm = np.stack([(np.arange(CLASS)[None, :] == w[:, None]) for w in rows]).astype(np.float32)
    return perm


PERM = place_tables()


def position():
    dp, ex = lax.axis_index("dp"), lax.axis_index("expert")
    return (lax.rem(ex // 2, 4), ex // 8, dp), lax.rem(ex, 2)


def device(co, core):
    return (co[2], co[1] * 8 + co[0] * 2 + core)


def shifted(co, axis, by):
    out = list(co)
    out[axis] = lax.rem(co[axis] + by, RING)
    return tuple(out)


def greet(co, core):
    barrier = pltpu.get_barrier_semaphore()
    for axis in (X, Y, Z):
        for by in (1, 2, 3):
            pl.semaphore_signal(
                barrier, inc=1, device_id=device(shifted(co, axis, by), core), device_id_type=MESH
            )
    pl.semaphore_signal(barrier, inc=1, device_id=device(co, 1 - core), device_id_type=MESH)


def remote(src, dst, send, recv, to):
    return pltpu.make_async_remote_copy(
        src_ref=src, dst_ref=dst, send_sem=send, recv_sem=recv, device_id=to, device_id_type=MESH
    )


def expert_of(co):
    return co[2] * 16 + co[1] * 4 + co[0]


def rows_at(start, size):
    return pl.ds(pl.multiple_of(start, 16), size)


def dot(a, b, over=((1,), (0,))):
    return lax.dot_general(a, b, (over, ((), ())), preferred_element_type=F32)


def segment(k):
    place = jnp.floor((k + 0.5) * (1.0 / BLOCK))
    half = jnp.where(k - place * BLOCK > TOK - 0.5, 1.0, 0.0)
    return place * CAP, half


def unit(n, dtype):
    return jnp.where(
        lax.broadcasted_iota(jnp.int32, (n, n), 0) == lax.broadcasted_iota(jnp.int32, (n, n), 1),
        1.0, 0.0,
    ).astype(dtype)


def routing_tile(routes, probs):
    lane = lax.broadcasted_iota(jnp.int32, (TOK, 128), 1).astype(F32)
    named = jnp.zeros((TOK, 128), F32)
    weight = jnp.zeros((TOK, 128), F32)
    for k in range(TOP):
        route = routes[:, k:k + 1]
        named = named + jnp.where(lane == route, 1.0, 0.0)
        weight = weight + jnp.where(lane == route + 64.0, probs[:, k:k + 1], 0.0)
    before = lax.broadcasted_iota(jnp.int32, (TOK, TOK), 0) > lax.broadcasted_iota(
        jnp.int32, (TOK, TOK), 1
    )
    rank = dot(jnp.where(before, 1.0, 0.0), named)
    meta = named * (rank + 1.0) + weight
    return jnp.concatenate([meta, meta], axis=0).astype(BF)


def kernel(
    tok, grd, routes_in, probs_in, perm_in, gate_w, up_w, down_w,
    token_grad, prob_grad, rows_out, delta_out, down_out,
    rows_t, rows_g, wgu, wd,
    gt0, gt1, gt2, gg0, gg1, gg2, st0, st1, st2, sg0, sg1, sg2, rt0, rt1, rt2, rg0, rg1, rg2,
    rr0, rr1, rr2, bs0, bs1, bs2, cs0, cs1, cs2,
    perm, delta, hid, gu,
    a1_s, a1_r, a2_s, a2_r, x_s, x_r, d_s, d_r, w_s, w_r, h_s, h_r,
    y_s, y_r, b2_s, b2_r, b1_s, b1_r, l_s, o_s, t_s,
):
    co, core = position()
    partner = device(co, 1 - core)
    gts, ggs = (gt0, gt1, gt2), (gg0, gg1, gg2)
    gat = (gts, ggs)
    sel = ((st0, st1, st2), (sg0, sg1, sg2))
    rec = ((rt0, rt1, rt2), (rg0, rg1, rg2))
    rrs, bss = (rr0, rr1, rr2), (bs0, bs1, bs2)
    css = (cs0, cs1, cs2)
    delta_o, hid_o, ptile = st0.at[0:CLASS], st2.at[0:CLASS, 0:HALF], st1.at[0:CLASS, 0:256]
    pk = gt0.at[0:CLASS, 768:896]
    uss = (st0.at[CLASS:576], st1.at[CLASS:576], st2.at[CLASS:576])
    at_of, half_of = (T_AT, G_AT), (T_HALF, G_HALF)
    gat_wide = (T_WIDE, G_HALF)
    sent = (T_SENT, G_HALF)
    outs = []

    def send(src, dst, s, r, to):
        c = remote(src, dst, s, r, to)
        c.start()
        outs.append(c)

    def arrive(ref, s, r):
        remote(ref, ref, s, r, partner).wait_recv()

    def settle():
        for c in outs:
            c.wait_send()
        outs.clear()

    H2 = 2 * HALF
    greet(co, core)
    loads = [
        pltpu.make_async_copy(gate_w.at[0], wgu.at[:, 0:HALF], l_s.at[0]),
        pltpu.make_async_copy(up_w.at[0], wgu.at[:, HALF:H2], l_s.at[1]),
        pltpu.make_async_copy(down_w.at[0], wd.at[0:HALF], l_s.at[2]),
        pltpu.make_async_copy(perm_in, perm, l_s.at[3]),
    ]
    for c in loads:
        c.start()
    eye = unit(TOK, F32)
    routes = dot(eye, routes_in[...].astype(F32), ((1,), (1,)))
    meta = routing_tile(routes, dot(eye, probs_in[...].astype(F32), ((1,), (1,))))

    def own_slot(p):
        a1, a2, a3 = ORDERS[p]
        return rows_at((co[a2] * 4 + co[a1]) * BLOCK, BLOCK)

    def pack(q, src):
        for p in range(3):
            at, h = at_of[q][p], half_of[q][p]
            both = jnp.concatenate(
                [src[:, at:at + h].astype(F32), src[:, at + h:at + 2 * h].astype(F32)], axis=0
            )
            gat[q][p][own_slot(p), 0:h] = both.astype(BF)
            if q == 0:
                gat[q][p][own_slot(p), h:h + 128] = meta

    def first(q):
        for p, (a1, a2, a3) in enumerate(ORDERS):
            view = gat[q][p].at[own_slot(p), 0:gat_wide[q][p]]
            for by in (1, 3, 2):
                send(
                    view, view, a1_s.at[q, p, by - 1], a1_r.at[q, p, by - 1],
                    device(shifted(co, a1, by), core),
                )

    pack(0, tok)
    pl.semaphore_wait(pltpu.get_barrier_semaphore(), 10)
    first(0)
    pack(1, grd)
    first(1)
    gathered = list(outs)
    outs.clear()
    send(gate_w.at[0], wgu.at[:, H2:H2 + HALF], w_s.at[0], w_r.at[0], partner)
    send(up_w.at[0], wgu.at[:, H2 + HALF:2 * H2], w_s.at[1], w_r.at[1], partner)
    send(down_w.at[0], wd.at[HALF:H2], w_s.at[2], w_r.at[2], partner)
    weights = list(outs)
    outs.clear()

    def part_of_line(q, p, b, which):
        return gat[q][p].at[rows_at(b * LINE + which * (LINE // 2), LINE // 2), 0:gat_wide[q][p]]

    def second_own(q):
        for p, (a1, a2, a3) in enumerate(ORDERS):
            for by in (1, 3, 2):
                theirs = rows_at((co[a2] * 4 + lax.rem(co[a1] + 4 - by, 4)) * BLOCK, BLOCK)
                arrive(
                    gat[q][p].at[theirs, 0:gat_wide[q][p]],
                    a1_s.at[q, p, by - 1], a1_r.at[q, p, by - 1],
                )
            up, down = device(shifted(co, a2, 1), core), device(shifted(co, a2, 3), core)
            for idx, which, to in ((0, 0, up), (3, 1, down), (1, 1, up), (4, 0, down)):
                ref = part_of_line(q, p, co[a2], which)
                send(ref, ref, a2_s.at[q, p, idx], a2_r.at[q, p, idx], to)
                gathered.append(outs.pop())

    def second_pass(q):
        for p, (a1, a2, a3) in enumerate(ORDERS):
            up, down = device(shifted(co, a2, 1), core), device(shifted(co, a2, 3), core)
            for got, idx, by, which, to in ((0, 2, 3, 0, up), (3, 5, 1, 1, down)):
                ref = part_of_line(q, p, lax.rem(co[a2] + by, 4), which)
                arrive(ref, a2_s.at[q, p, got], a2_r.at[q, p, got])
                send(ref, ref, a2_s.at[q, p, idx], a2_r.at[q, p, idx], to)
                gathered.append(outs.pop())

    def second_wait(q, p):
        a1, a2, a3 = ORDERS[p]
        for idx, by, which in ((1, 3, 1), (4, 1, 0), (2, 2, 0), (5, 2, 1)):
            arrive(
                part_of_line(q, p, lax.rem(co[a2] + by, 4), which),
                a2_s.at[q, p, idx], a2_r.at[q, p, idx],
            )

    k_row = lax.broadcasted_iota(jnp.int32, (1, PLANE), 1).astype(F32)
    place_row, half_row = segment(k_row)
    top = half_row < 0.5
    slot = lax.broadcasted_iota(jnp.int32, (SLOTS, PLANE), 0).astype(F32)

    def wanted(p):
        a1, a2, a3 = ORDERS[p]
        h = T_HALF[p]
        line = lax.broadcasted_iota(jnp.int32, (8, 128), 0)
        lane = lax.broadcasted_iota(jnp.int32, (8, 128), 1)
        name = jnp.full((8, 128), -1, jnp.int32)
        for by in range(4):
            name = jnp.where(line == by, expert_of(shifted(co, a3, by)), name)
        pick = jnp.where(lane == name, 1.0, 0.0).astype(BF)
        val = dot(pick, gts[p][:, h:h + 128], ((1,), (1,)))
        return jnp.where(val > 0.5, val - 1.0 + place_row, -1.0)

    def choose(q, p, want):
        a1, a2, a3 = ORDERS[p]
        picks = []
        for by in (1, 3, 2, 0):
            row = want[by:by + 1, :]
            picks.append(jnp.where(slot == jnp.where(top, row, -1.0), 1.0, 0.0).astype(BF))
            picks.append(jnp.where(slot == jnp.where(top, -1.0, row), 1.0, 0.0).astype(BF))
        w = sent[q][p]
        got = dot(jnp.concatenate(picks, axis=0), gat[q][p][:, 0:w]).astype(BF)
        mine = rows_at(co[a3] * 192, 192)
        for n, by in enumerate((1, 3, 2)):
            rows = slice(n * 192, n * 192 + 192)
            sel[q][p][rows, :] = got[rows]
            send(
                sel[q][p].at[rows], rec[q][p].at[mine, 0:w],
                x_s.at[q, p, by - 1], x_r.at[q, p, by - 1], device(shifted(co, a3, by), core),
            )
        rec[q][p][mine, 0:w] = got[576:768]

    def reorder(q, p, out):
        a1, a2, a3 = ORDERS[p]
        w = sent[q][p]
        for by in (1, 3, 2):
            ref = rec[q][p].at[rows_at(lax.rem(co[a3] + 4 - by, 4) * 192, 192), 0:w]
            arrive(ref, x_s.at[q, p, by - 1], x_r.at[q, p, by - 1])
        at, h = at_of[q][p], half_of[q][p]
        for n in range(2):
            full = jnp.concatenate(
                [rec[q][p][b * 192 + n * 96:b * 192 + n * 96 + 96, 0:w] for b in range(4)], axis=0
            )
            if p > 0:
                full = dot(perm[p - 1], full).astype(BF)
            out[0:CLASS, at + n * h:at + n * h + h] = full[:, 0:h]
            if q == 0 and p == 2 and n == 0:
                pk[...] = full[:, h:h + 128]
        cols = slice(at, at + 2 * h)
        if q == 0:
            c = pltpu.make_async_copy(rows_t.at[:, cols], rows_out.at[0:CLASS, cols], t_s.at[p])
            c.start()
            stores.append(c)
        there = rows_out if q == 0 else rows_g
        send(
            out.at[0:CLASS, cols], there.at[CLASS:ROWS, cols], d_s.at[q, p], d_r.at[q, p], partner
        )

    stores = []
    second_own(0)
    second_pass(0)
    second_own(1)
    wants = []
    for p in range(3):
        second_wait(0, p)
        wants.append(wanted(p))
        choose(0, p, wants[p])
        if p == 0:
            second_pass(1)
    for p in range(3):
        second_wait(1, p)
        choose(1, p, wants[p])
    for c in gathered:
        c.wait_send()
    exchanged = list(outs)
    outs.clear()
    code = lax.broadcasted_iota(jnp.int32, (LINE, PLANE), 1).astype(F32)
    k_col = lax.broadcasted_iota(jnp.int32, (PLANE, 128), 0).astype(F32)
    place_col, half_col = segment(k_col)
    for p, (a1, a2, a3) in enumerate(ORDERS):
        line = lax.broadcasted_iota(jnp.int32, (128, 128), 0)
        lane = lax.broadcasted_iota(jnp.int32, (128, 128), 1)
        name = jnp.full((128, 128), -1, jnp.int32)
        for b in range(4):
            at_b = list(co)
            at_b[a3] = b
            name = jnp.where(line == b, expert_of(at_b), name)
        pick = jnp.where(lane == name, 1.0, 0.0).astype(BF)
        val = dot(gts[p][:, T_HALF[p]:T_HALF[p] + 128], pick, ((1,), (1,)))
        lane = lax.broadcasted_iota(jnp.int32, (PLANE, 128), 1).astype(F32)
        spot = jnp.where(
            val > 0.5, val - 1.0 + place_col + lane * 192.0 + half_col * 96.0, -1.0
        )
        for r in range(0, PLANE, LINE):
            put = jnp.zeros((LINE, PLANE), F32)
            for b in range(4):
                put = jnp.where(code == spot[r:r + LINE, b:b + 1], 1.0, put)
            ggs[p][r:r + LINE, :] = put.astype(BF)
    for c in loads:
        c.wait()
    for p in range(3):
        reorder(0, p, rows_t)
    gu[:, 0:H2] = dot(rows_t[...], wgu[:, 0:H2])
    arrive(wgu.at[:, H2:H2 + HALF], w_s.at[0], w_r.at[0])
    arrive(wgu.at[:, H2 + HALF:2 * H2], w_s.at[1], w_r.at[1])
    arrive(wd.at[HALF:H2], w_s.at[2], w_r.at[2])
    gu[:, H2:2 * H2] = dot(rows_t[...], wgu[:, H2:2 * H2])
    for p in range(3):
        reorder(1, p, rows_g)

    for c in exchanged:
        c.wait_send()
    lane = lax.broadcasted_iota(jnp.int32, (CLASS, 128), 1)
    weight = jnp.sum(
        jnp.where(lane == 64 + expert_of(co), pk[...].astype(F32), 0.0), axis=1, keepdims=True
    )
    raws = [
        dot(rows_g[0:CLASS, :], wd[n * HALF:n * HALF + HALF, :], ((1,), (1,))) for n in range(2)
    ]
    for r in range(0, CLASS, SLOTS):
        rows = slice(r, r + SLOTS)
        prob = jnp.zeros((SLOTS, 1), F32)
        for n, (dl, hd) in enumerate(((delta, hid), (delta_o, hid_o))):
            gate, up = gu[rows, n * H2:n * H2 + HALF], gu[rows, n * H2 + HALF:n * H2 + H2]
            grad = raws[n][rows]
            sig = jax.nn.sigmoid(gate)
            active = gate * sig
            hidden = active * up
            scaled = weight[rows] * grad
            dl[rows, 0:HALF] = (scaled * up * sig * (1.0 + gate * (1.0 - sig))).astype(BF)
            dl[rows, HALF:H2] = (scaled * active).astype(BF)
            hd[rows, :] = (weight[rows] * hidden).astype(BF)
            prob = prob + jnp.sum(hidden * grad, axis=1, keepdims=True).astype(BF).astype(F32)
        prob = jnp.where(lane[rows] == expert_of(co), prob, 0.0)
        prob_hi = prob.astype(BF)
        ptile[rows, 0:128] = prob_hi
        ptile[rows, 128:256] = (prob - prob_hi.astype(F32)).astype(BF)

    def piece(p, c):
        h = CUT if c == 0 else T_HALF[p] - CUT
        return T_AT[p] + c * 2 * CUT, h, slice(c * CUT, c * CUT + h + (128 if (p, c) == (2, 1) else 0))

    def input_part(p, c):
        a1, a2, a3 = ORDERS[p]
        at, h, cols = piece(p, c)
        if p == 0:
            own, other = delta[...], delta_o[...]
        else:
            if c == 0:
                rec[1][p][0:CLASS, :] = dot(perm[p - 1], delta[...], ((0,), (0,))).astype(BF)
                rec[1][p][CLASS:ROWS, :] = dot(perm[p - 1], delta_o[...], ((0,), (0,))).astype(BF)
            own, other = rec[1][p][0:CLASS, :], rec[1][p][CLASS:ROWS, :]
        if (p, c) == (2, 1):
            tiles = dot(perm[p - 1], ptile[...], ((0,), (0,))).astype(BF)
        w = slice(at, at + 2 * h)
        both = (
            dot(own, wgu[w, 0:H2], ((1,), (1,))) + dot(other, wgu[w, H2:2 * H2], ((1,), (1,)))
        ).astype(BF)
        for n in range(2):
            val = both[:, n * h:n * h + h]
            if (p, c) == (2, 1):
                val = jnp.concatenate([val, tiles[:, n * 128:n * 128 + 128]], axis=1)
            for b in range(4):
                rec[0][p][b * 192 + n * 96:b * 192 + n * 96 + 96, cols] = val[b * 96:b * 96 + 96, :]
        for by in (1, 3, 2):
            to = shifted(co, a3, by)
            send(
                rec[0][p].at[rows_at(to[a3] * 192, 192), cols],
                rrs[p].at[rows_at(co[a3] * 192, 192), cols],
                y_s.at[c, p, by - 1], y_r.at[c, p, by - 1], device(to, core),
            )
        mine = rows_at(co[a3] * 192, 192)
        rrs[p][mine, cols] = rec[0][p][mine, cols]

    for c in range(2):
        for p in range(3):
            input_part(p, c)
    send(delta_o, delta_out.at[CLASS:ROWS], h_s.at[0], h_r.at[0], partner)
    send(hid_o, hid.at[CLASS:ROWS], h_s.at[1], h_r.at[1], partner)
    c = pltpu.make_async_copy(delta, delta_out.at[0:CLASS], t_s.at[3])
    c.start()
    stores.append(c)

    stage_d = (rg0.at[0:CLASS, 0:STEP], rg0.at[CLASS:ROWS, 0:STEP])

    def down_out_copy(n, cols):
        return pltpu.make_async_copy(stage_d[n], down_out.at[0, :, cols], o_s.at[n])

    def down_step(i, carry):
        for n in range(2):
            @pl.when(i > 0)
            def _():
                down_out_copy(n, slice(0, STEP)).wait()
            cols = pl.ds(pl.multiple_of((2 * i + n) * STEP, STEP), STEP)
            stage_d[n][...] = dot(hid[...], rows_g[:, cols], ((0,), (0,))).astype(BF)
            down_out_copy(n, cols).start()
        return carry

    sums = gts

    def relay(c):
        for p, (a1, a2, a3) in enumerate(ORDERS):
            cols = piece(p, c)[2]
            for by in (1, 3, 2):
                ref = rrs[p].at[rows_at(lax.rem(co[a3] + 4 - by, 4) * 192, 192), cols]
                arrive(ref, y_s.at[c, p, by - 1], y_r.at[c, p, by - 1])
            sums[p][:, cols] = dot(ggs[p][...], rrs[p][:, cols]).astype(BF)
            for by in (1, 3, 2):
                to = shifted(co, a2, by)
                send(
                    sums[p].at[rows_at(to[a2] * LINE, LINE), cols], bss[p].at[by - 1, :, cols],
                    b2_s.at[c, p, by - 1], b2_r.at[c, p, by - 1], device(to, core),
                )

    def line_sum(c):
        for p, (a1, a2, a3) in enumerate(ORDERS):
            cols = piece(p, c)[2]
            total = sums[p][rows_at(co[a2] * LINE, LINE), cols].astype(F32)
            for by in (1, 3, 2):
                arrive(bss[p].at[by - 1, :, cols], b2_s.at[c, p, by - 1], b2_r.at[c, p, by - 1])
                total = total + bss[p][by - 1, :, cols].astype(F32)
            uss[p][:, cols] = total.astype(BF)
            for by in (1, 3, 2):
                to = shifted(co, a1, by)
                send(
                    uss[p].at[rows_at(to[a1] * BLOCK, BLOCK), cols], css[p].at[by - 1, :, cols],
                    b1_s.at[c, p, by - 1], b1_r.at[c, p, by - 1], device(to, core),
                )

    def finish(c):
        for p, (a1, a2, a3) in enumerate(ORDERS):
            at, h, cols = piece(p, c)
            total = uss[p][rows_at(co[a1] * BLOCK, BLOCK), cols].astype(F32)
            for by in (1, 3, 2):
                arrive(css[p].at[by - 1, :, cols], b1_s.at[c, p, by - 1], b1_r.at[c, p, by - 1])
                total = total + css[p][by - 1, :, cols].astype(F32)
            token_grad[:, at:at + h] = total[0:TOK, 0:h].astype(BF)
            token_grad[:, at + h:at + 2 * h] = total[TOK:, 0:h].astype(BF)
            if (p, c) == (2, 1):
                per = total[0:TOK, h:h + 128] + total[TOK:, h:h + 128]
                lane = lax.broadcasted_iota(jnp.int32, (TOK, 128), 1).astype(F32)
                spot = lax.broadcasted_iota(jnp.int32, (TOK, TOP), 1)
                grad = jnp.zeros((TOK, TOP), F32)
                for k in range(TOP):
                    one = jnp.sum(
                        jnp.where(lane == routes[:, k:k + 1], per, 0.0), axis=1, keepdims=True
                    )
                    grad = jnp.where(spot == k, one, grad)
                prob_grad[...] = lax.dot_general(
                    unit(TOP, F32), grad, (((1,), (1,)), ((), ())),
                    preferred_element_type=F32, precision=lax.Precision.HIGHEST,
                )

    relay(0)
    for p in range(3):
        cols = slice(G_AT[p], G_AT[p] + 2 * G_HALF[p])
        arrive(rows_g.at[CLASS:ROWS, cols], d_s.at[1, p], d_r.at[1, p])
    arrive(hid.at[CLASS:ROWS], h_s.at[1], h_r.at[1])
    lax.fori_loop(0, 2, down_step, 0)
    relay(1)
    line_sum(0)
    lax.fori_loop(2, 4, down_step, 0)
    line_sum(1)
    finish(0)
    finish(1)
    for n in range(2):
        down_out_copy(n, slice(0, STEP)).wait()
    for p in range(3):
        cols = slice(T_AT[p], T_AT[p] + 2 * T_HALF[p])
        arrive(rows_out.at[CLASS:ROWS, cols], d_s.at[0, p], d_r.at[0, p])
    arrive(delta_out.at[CLASS:ROWS], h_s.at[0], h_r.at[0])
    for c in stores:
        c.wait()
    for c in weights:
        c.wait_send()
    settle()


def weight_kernel(token, prob, rows, delta, down, token_out, prob_out, gate_out, up_out, down_out):
    grads = dot(rows[...], delta[...], ((0,), (0,))).astype(BF)
    gate_out[0] = grads[:, 0:HALF]
    up_out[0] = grads[:, HALF:2 * HALF]
    down_out[...] = down[...]

    @pl.when(pl.program_id(0) == 0)
    def _():
        token_out[...] = token[...]
        prob_out[...] = prob[...]


def on_device(tokens, out_grad, routes, gate_probs, gate_weight, up_weight, down_weight):
    vmem = pl.BlockSpec(memory_space=pltpu.VMEM)
    anywhere = pl.BlockSpec(memory_space=pl.ANY)
    dma = pltpu.SemaphoreType.DMA
    shapes = [(CLASS, D), (ROWS, D), (D, 4 * HALF), (2 * HALF, D)]
    shapes += [(PLANE, 896), (PLANE, 768), (PLANE, 768)] + [(PLANE, 768)] * 3
    shapes += [(576, w) for w in T_SENT] + [(576, w) for w in G_HALF]
    shapes += [(ROWS, w) for w in T_SENT] + [(ROWS, w) for w in (640, 768, 768)]
    shapes += [(ROWS, w) for w in BACK]
    shapes += [(3, LINE, w) for w in BACK]
    shapes += [(3, BLOCK, w) for w in BACK]
    shapes += [PERM.shape, (CLASS, 2 * HALF), (ROWS, HALF)]
    scratch = [pltpu.VMEM(s, BF) for s in shapes] + [pltpu.VMEM((CLASS, 4 * HALF), F32)]
    for s in ((2, 3, 3), (2, 3, 6), (2, 3, 3), (2, 3), (3,), (2,)) + ((2, 3, 3),) * 3:
        scratch += [dma(s), dma(s)]
    scratch += [dma((4,)), dma((2,)), dma((4,))]
    token_shape = jax.ShapeDtypeStruct((TOK, D), BF)
    prob_shape = jax.ShapeDtypeStruct((TOP, TOK), F32)
    wide_shape = jax.ShapeDtypeStruct((1, D, HALF), BF)
    down_shape = jax.ShapeDtypeStruct((1, HALF, D), BF)
    results = pl.pallas_call(
        kernel,
        out_shape=(
            token_shape,
            prob_shape,
            jax.ShapeDtypeStruct((ROWS, D), BF),
            jax.ShapeDtypeStruct((ROWS, 2 * HALF), BF),
            down_shape,
        ),
        in_specs=[vmem] * 4 + [anywhere] * 4,
        out_specs=(vmem, vmem, anywhere, anywhere, anywhere),
        scratch_shapes=scratch,
        compiler_params=pltpu.CompilerParams(
            collective_id=1, has_side_effects=True, vmem_limit_bytes=65400 * 2**10
        ),
        name="routed_backward",
    )(
        tokens, out_grad, routes.T, gate_probs.T, jnp.asarray(PERM, BF),
        gate_weight, up_weight, down_weight,
    )
    whole = [pl.BlockSpec((TOK, D), lambda i: (0, 0)), pl.BlockSpec((TOP, TOK), lambda i: (0, 0))]
    tall = pl.BlockSpec((1, STEP, HALF), lambda i: (0, i, 0))
    flat = pl.BlockSpec((1, HALF, STEP), lambda i: (0, 0, i))
    token_grad, prob_grad, gate_grad, up_grad, down_grad = pl.pallas_call(
        weight_kernel,
        grid=(D // STEP,),
        out_shape=(token_shape, prob_shape, wide_shape, wide_shape, down_shape),
        in_specs=whole + [
            pl.BlockSpec((ROWS, STEP), lambda i: (0, i)),
            pl.BlockSpec((ROWS, 2 * HALF), lambda i: (0, 0)),
            flat,
        ],
        out_specs=whole + [tall, tall, flat],
        compiler_params=pltpu.CompilerParams(vmem_limit_bytes=62 * 2**20),
        name="weight_grads",
    )(*results)
    return token_grad, prob_grad.T, gate_grad, up_grad, down_grad


def solution(mesh):
    two, three = P(("dp", "expert"), None), P(("dp", "expert"), None, None)
    return jax.shard_map(
        on_device,
        mesh=mesh,
        in_specs=(two, two, two, two, three, three, three),
        out_specs=(two, two, three, three, three),
        check_vma=False,
    )
```

```python
import numpy as np
import jax
import jax.numpy as jnp
from jax import lax
from jax.sharding import PartitionSpec as P
from jax.experimental import pallas as pl
from jax.experimental.pallas import tpu as pltpu

MESH = pl.DeviceIdType.MESH
BF = jnp.bfloat16
F32 = jnp.float32
D = 4096
HALF = 384
TOK = 24
TOP = 8
CAP = 6
RING = 4
SLOTS = 16 * CAP
CLASS = RING * SLOTS
ROWS = 2 * CLASS
BLOCK = 2 * TOK
PLANE = 16 * BLOCK
LINE = 4 * BLOCK
STEP = 512
TALL = 1024
X, Y, Z = 0, 1, 2
ORDERS = ((Z, Y, X), (X, Z, Y), (Y, X, Z))
T_AT, T_HALF = (0, 1536, 2816), (768, 640, 640)
G_AT, G_HALF = (0, 1280, 2816), (640, 768, 640)
T_WIDE = (896, 768, 768)
T_SENT = (768, 640, 768)
BACK = (768, 640, 768)
CUT = 384


def place_tables():
    i = np.arange(CLASS)
    x, y, z, r = i // 96, i // 24 % 4, i // 6 % 4, i % 6
    rows = (y * 96 + (z * 4 + x) * 6 + r, z * 96 + (x * 4 + y) * 6 + r)
    perm = np.stack([(np.arange(CLASS)[None, :] == w[:, None]) for w in rows]).astype(np.float32)
    return perm


PERM = place_tables()


def position():
    dp, ex = lax.axis_index("dp"), lax.axis_index("expert")
    return (lax.rem(ex // 2, 4), ex // 8, dp), lax.rem(ex, 2)


def device(co, core):
    return (co[2], co[1] * 8 + co[0] * 2 + core)


def shifted(co, axis, by):
    out = list(co)
    out[axis] = lax.rem(co[axis] + by, RING)
    return tuple(out)


def greet(co, core):
    barrier = pltpu.get_barrier_semaphore()
    for axis in (X, Y, Z):
        for by in (1, 2, 3):
            pl.semaphore_signal(
                barrier, inc=1, device_id=device(shifted(co, axis, by), core), device_id_type=MESH
            )
    pl.semaphore_signal(barrier, inc=1, device_id=device(co, 1 - core), device_id_type=MESH)


def remote(src, dst, send, recv, to):
    return pltpu.make_async_remote_copy(
        src_ref=src, dst_ref=dst, send_sem=send, recv_sem=recv, device_id=to, device_id_type=MESH
    )


def expert_of(co):
    return co[2] * 16 + co[1] * 4 + co[0]


def rows_at(start, size):
    return pl.ds(pl.multiple_of(start, 16), size)


def dot(a, b, over=((1,), (0,))):
    return lax.dot_general(a, b, (over, ((), ())), preferred_element_type=F32)


def segment(k):
    place = jnp.floor((k + 0.5) * (1.0 / BLOCK))
    half = jnp.where(k - place * BLOCK > TOK - 0.5, 1.0, 0.0)
    return place * CAP, half


def unit(n, dtype):
    return jnp.where(
        lax.broadcasted_iota(jnp.int32, (n, n), 0) == lax.broadcasted_iota(jnp.int32, (n, n), 1),
        1.0, 0.0,
    ).astype(dtype)


def routing_tile(routes, probs):
    lane = lax.broadcasted_iota(jnp.int32, (TOK, 128), 1).astype(F32)
    named = jnp.zeros((TOK, 128), F32)
    weight = jnp.zeros((TOK, 128), F32)
    for k in range(TOP):
        route = routes[:, k:k + 1]
        named = named + jnp.where(lane == route, 1.0, 0.0)
        weight = weight + jnp.where(lane == route + 64.0, probs[:, k:k + 1], 0.0)
    before = lax.broadcasted_iota(jnp.int32, (TOK, TOK), 0) > lax.broadcasted_iota(
        jnp.int32, (TOK, TOK), 1
    )
    rank = dot(jnp.where(before, 1.0, 0.0), named)
    meta = named * (rank + 1.0) + weight
    return jnp.concatenate([meta, meta], axis=0).astype(BF)


def kernel(
    tok, grd, routes_in, probs_in, perm_in, gate_w, up_w, down_w,
    token_grad, prob_grad, rows_out, delta_out, down_out,
    rows_t, rows_g, wgu, wd,
    gt0, gt1, gt2, gg0, gg1, gg2, st0, st1, st2, sg0, sg1, sg2, rt0, rt1, rt2, rg0, rg1, rg2,
    rr0, rr1, rr2, bs0, bs1, bs2, cs0, cs1, cs2,
    perm, delta, hid, gu,
    a1_s, a1_r, a2_s, a2_r, x_s, x_r, d_s, d_r, w_s, w_r, h_s, h_r,
    y_s, y_r, b2_s, b2_r, b1_s, b1_r, l_s, o_s, t_s,
):
    co, core = position()
    partner = device(co, 1 - core)
    gts, ggs = (gt0, gt1, gt2), (gg0, gg1, gg2)
    gat = (gts, ggs)
    sel = ((st0, st1, st2), (sg0, sg1, sg2))
    rec = ((rt0, rt1, rt2), (rg0, rg1, rg2))
    rrs, bss = (rr0, rr1, rr2), (bs0, bs1, bs2)
    css = (cs0, cs1, cs2)
    delta_o, hid_o, ptile = st0.at[0:CLASS], st2.at[0:CLASS, 0:HALF], st1.at[0:CLASS, 0:256]
    pk = gt0.at[0:CLASS, 768:896]
    uss = (st0.at[CLASS:576], st1.at[CLASS:576], st2.at[CLASS:576])
    at_of, half_of = (T_AT, G_AT), (T_HALF, G_HALF)
    gat_wide = (T_WIDE, G_HALF)
    sent = (T_SENT, G_HALF)
    outs = []

    def send(src, dst, s, r, to):
        c = remote(src, dst, s, r, to)
        c.start()
        outs.append(c)

    def arrive(ref, s, r):
        remote(ref, ref, s, r, partner).wait_recv()

    def settle():
        for c in outs:
            c.wait_send()
        outs.clear()

    H2 = 2 * HALF
    greet(co, core)
    loads = [
        pltpu.make_async_copy(gate_w.at[0], wgu.at[:, 0:HALF], l_s.at[0]),
        pltpu.make_async_copy(up_w.at[0], wgu.at[:, HALF:H2], l_s.at[1]),
        pltpu.make_async_copy(down_w.at[0], wd.at[0:HALF], l_s.at[2]),
        pltpu.make_async_copy(perm_in, perm, l_s.at[3]),
    ]
    for c in loads:
        c.start()
    eye = unit(TOK, F32)
    routes = dot(eye, routes_in[...].astype(F32), ((1,), (1,)))
    meta = routing_tile(routes, dot(eye, probs_in[...].astype(F32), ((1,), (1,))))

    def own_slot(p):
        a1, a2, a3 = ORDERS[p]
        return rows_at((co[a2] * 4 + co[a1]) * BLOCK, BLOCK)

    def pack(q, src):
        for p in range(3):
            at, h = at_of[q][p], half_of[q][p]
            both = jnp.concatenate(
                [src[:, at:at + h].astype(F32), src[:, at + h:at + 2 * h].astype(F32)], axis=0
            )
            gat[q][p][own_slot(p), 0:h] = both.astype(BF)
            if q == 0:
                gat[q][p][own_slot(p), h:h + 128] = meta

    def first(q):
        for p, (a1, a2, a3) in enumerate(ORDERS):
            view = gat[q][p].at[own_slot(p), 0:gat_wide[q][p]]
            for by in (1, 3, 2):
                send(
                    view, view, a1_s.at[q, p, by - 1], a1_r.at[q, p, by - 1],
                    device(shifted(co, a1, by), core),
                )

    pack(0, tok)
    pl.semaphore_wait(pltpu.get_barrier_semaphore(), 10)
    first(0)
    pack(1, grd)
    first(1)
    gathered = list(outs)
    outs.clear()
    send(gate_w.at[0], wgu.at[:, H2:H2 + HALF], w_s.at[0], w_r.at[0], partner)
    send(up_w.at[0], wgu.at[:, H2 + HALF:2 * H2], w_s.at[1], w_r.at[1], partner)
    send(down_w.at[0], wd.at[HALF:H2], w_s.at[2], w_r.at[2], partner)
    weights = list(outs)
    outs.clear()

    def part_of_line(q, p, b, which):
        return gat[q][p].at[rows_at(b * LINE + which * (LINE // 2), LINE // 2), 0:gat_wide[q][p]]

    def second_own(q):
        for p, (a1, a2, a3) in enumerate(ORDERS):
            for by in (1, 3, 2):
                theirs = rows_at((co[a2] * 4 + lax.rem(co[a1] + 4 - by, 4)) * BLOCK, BLOCK)
                arrive(
                    gat[q][p].at[theirs, 0:gat_wide[q][p]],
                    a1_s.at[q, p, by - 1], a1_r.at[q, p, by - 1],
                )
            up, down = device(shifted(co, a2, 1), core), device(shifted(co, a2, 3), core)
            for idx, which, to in ((0, 0, up), (3, 1, down), (1, 1, up), (4, 0, down)):
                ref = part_of_line(q, p, co[a2], which)
                send(ref, ref, a2_s.at[q, p, idx], a2_r.at[q, p, idx], to)
                gathered.append(outs.pop())

    def second_pass(q):
        for p, (a1, a2, a3) in enumerate(ORDERS):
            up, down = device(shifted(co, a2, 1), core), device(shifted(co, a2, 3), core)
            for got, idx, by, which, to in ((0, 2, 3, 0, up), (3, 5, 1, 1, down)):
                ref = part_of_line(q, p, lax.rem(co[a2] + by, 4), which)
                arrive(ref, a2_s.at[q, p, got], a2_r.at[q, p, got])
                send(ref, ref, a2_s.at[q, p, idx], a2_r.at[q, p, idx], to)
                gathered.append(outs.pop())

    def second_wait(q, p):
        a1, a2, a3 = ORDERS[p]
        for idx, by, which in ((1, 3, 1), (4, 1, 0), (2, 2, 0), (5, 2, 1)):
            arrive(
                part_of_line(q, p, lax.rem(co[a2] + by, 4), which),
                a2_s.at[q, p, idx], a2_r.at[q, p, idx],
            )

    k_row = lax.broadcasted_iota(jnp.int32, (1, PLANE), 1).astype(F32)
    place_row, half_row = segment(k_row)
    top = half_row < 0.5
    slot = lax.broadcasted_iota(jnp.int32, (SLOTS, PLANE), 0).astype(F32)

    def wanted(p):
        a1, a2, a3 = ORDERS[p]
        h = T_HALF[p]
        line = lax.broadcasted_iota(jnp.int32, (8, 128), 0)
        lane = lax.broadcasted_iota(jnp.int32, (8, 128), 1)
        name = jnp.full((8, 128), -1, jnp.int32)
        for by in range(4):
            name = jnp.where(line == by, expert_of(shifted(co, a3, by)), name)
        pick = jnp.where(lane == name, 1.0, 0.0).astype(BF)
        val = dot(pick, gts[p][:, h:h + 128], ((1,), (1,)))
        return jnp.where(val > 0.5, val - 1.0 + place_row, -1.0)

    def choose(q, p, want):
        a1, a2, a3 = ORDERS[p]
        picks = []
        for by in (1, 3, 2, 0):
            row = want[by:by + 1, :]
            picks.append(jnp.where(slot == jnp.where(top, row, -1.0), 1.0, 0.0).astype(BF))
            picks.append(jnp.where(slot == jnp.where(top, -1.0, row), 1.0, 0.0).astype(BF))
        w = sent[q][p]
        got = dot(jnp.concatenate(picks, axis=0), gat[q][p][:, 0:w]).astype(BF)
        mine = rows_at(co[a3] * 192, 192)
        for n, by in enumerate((1, 3, 2)):
            rows = slice(n * 192, n * 192 + 192)
            sel[q][p][rows, :] = got[rows]
            send(
                sel[q][p].at[rows], rec[q][p].at[mine, 0:w],
                x_s.at[q, p, by - 1], x_r.at[q, p, by - 1], device(shifted(co, a3, by), core),
            )
        rec[q][p][mine, 0:w] = got[576:768]

    def reorder(q, p, out):
        a1, a2, a3 = ORDERS[p]
        w = sent[q][p]
        for by in (1, 3, 2):
            ref = rec[q][p].at[rows_at(lax.rem(co[a3] + 4 - by, 4) * 192, 192), 0:w]
            arrive(ref, x_s.at[q, p, by - 1], x_r.at[q, p, by - 1])
        at, h = at_of[q][p], half_of[q][p]
        for n in range(2):
            full = jnp.concatenate(
                [rec[q][p][b * 192 + n * 96:b * 192 + n * 96 + 96, 0:w] for b in range(4)], axis=0
            )
            if p > 0:
                full = dot(perm[p - 1], full).astype(BF)
            out[0:CLASS, at + n * h:at + n * h + h] = full[:, 0:h]
            if q == 0 and p == 2 and n == 0:
                pk[...] = full[:, h:h + 128]
        cols = slice(at, at + 2 * h)
        if q == 0:
            c = pltpu.make_async_copy(rows_t.at[:, cols], rows_out.at[0:CLASS, cols], t_s.at[p])
            c.start()
            stores.append(c)
        there = rows_out if q == 0 else rows_g
        send(
            out.at[0:CLASS, cols], there.at[CLASS:ROWS, cols], d_s.at[q, p], d_r.at[q, p], partner
        )

    stores = []
    second_own(0)
    second_pass(0)
    second_own(1)
    wants = []
    for p in range(3):
        second_wait(0, p)
        wants.append(wanted(p))
        choose(0, p, wants[p])
        if p == 0:
            second_pass(1)
    for p in range(3):
        second_wait(1, p)
        choose(1, p, wants[p])
    for c in gathered:
        c.wait_send()
    exchanged = list(outs)
    outs.clear()
    code = lax.broadcasted_iota(jnp.int32, (LINE, PLANE), 1).astype(F32)
    k_col = lax.broadcasted_iota(jnp.int32, (PLANE, 128), 0).astype(F32)
    place_col, half_col = segment(k_col)
    for p, (a1, a2, a3) in enumerate(ORDERS):
        line = lax.broadcasted_iota(jnp.int32, (128, 128), 0)
        lane = lax.broadcasted_iota(jnp.int32, (128, 128), 1)
        name = jnp.full((128, 128), -1, jnp.int32)
        for b in range(4):
            at_b = list(co)
            at_b[a3] = b
            name = jnp.where(line == b, expert_of(at_b), name)
        pick = jnp.where(lane == name, 1.0, 0.0).astype(BF)
        val = dot(gts[p][:, T_HALF[p]:T_HALF[p] + 128], pick, ((1,), (1,)))
        lane = lax.broadcasted_iota(jnp.int32, (PLANE, 128), 1).astype(F32)
        spot = jnp.where(
            val > 0.5, val - 1.0 + place_col + lane * 192.0 + half_col * 96.0, -1.0
        )
        for r in range(0, PLANE, LINE):
            put = jnp.zeros((LINE, PLANE), F32)
            for b in range(4):
                put = jnp.where(code == spot[r:r + LINE, b:b + 1], 1.0, put)
            ggs[p][r:r + LINE, :] = put.astype(BF)
    for c in loads:
        c.wait()
    for p in range(3):
        reorder(0, p, rows_t)
    gu[:, 0:H2] = dot(rows_t[...], wgu[:, 0:H2])
    arrive(wgu.at[:, H2:H2 + HALF], w_s.at[0], w_r.at[0])
    arrive(wgu.at[:, H2 + HALF:2 * H2], w_s.at[1], w_r.at[1])
    arrive(wd.at[HALF:H2], w_s.at[2], w_r.at[2])
    gu[:, H2:2 * H2] = dot(rows_t[...], wgu[:, H2:2 * H2])
    for p in range(3):
        reorder(1, p, rows_g)

    for c in exchanged:
        c.wait_send()
    lane = lax.broadcasted_iota(jnp.int32, (CLASS, 128), 1)
    weight = jnp.sum(
        jnp.where(lane == 64 + expert_of(co), pk[...].astype(F32), 0.0), axis=1, keepdims=True
    )
    raws = [
        dot(rows_g[0:CLASS, :], wd[n * HALF:n * HALF + HALF, :], ((1,), (1,))) for n in range(2)
    ]
    for r in range(0, CLASS, SLOTS):
        rows = slice(r, r + SLOTS)
        prob = jnp.zeros((SLOTS, 1), F32)
        for n, (dl, hd) in enumerate(((delta, hid), (delta_o, hid_o))):
            gate, up = gu[rows, n * H2:n * H2 + HALF], gu[rows, n * H2 + HALF:n * H2 + H2]
            grad = raws[n][rows]
            sig = jax.nn.sigmoid(gate)
            active = gate * sig
            hidden = active * up
            scaled = weight[rows] * grad
            dl[rows, 0:HALF] = (scaled * up * sig * (1.0 + gate * (1.0 - sig))).astype(BF)
            dl[rows, HALF:H2] = (scaled * active).astype(BF)
            hd[rows, :] = (weight[rows] * hidden).astype(BF)
            prob = prob + jnp.sum(hidden * grad, axis=1, keepdims=True).astype(BF).astype(F32)
        prob = jnp.where(lane[rows] == expert_of(co), prob, 0.0)
        prob_hi = prob.astype(BF)
        ptile[rows, 0:128] = prob_hi
        ptile[rows, 128:256] = (prob - prob_hi.astype(F32)).astype(BF)

    def piece(p, c):
        h = CUT if c == 0 else T_HALF[p] - CUT
        return T_AT[p] + c * 2 * CUT, h, slice(c * CUT, c * CUT + h + (128 if (p, c) == (2, 1) else 0))

    def input_part(p, c):
        a1, a2, a3 = ORDERS[p]
        at, h, cols = piece(p, c)
        if p == 0:
            own, other = delta[...], delta_o[...]
        else:
            if c == 0:
                rec[1][p][0:CLASS, :] = dot(perm[p - 1], delta[...], ((0,), (0,))).astype(BF)
                rec[1][p][CLASS:ROWS, :] = dot(perm[p - 1], delta_o[...], ((0,), (0,))).astype(BF)
            own, other = rec[1][p][0:CLASS, :], rec[1][p][CLASS:ROWS, :]
        if (p, c) == (2, 1):
            tiles = dot(perm[p - 1], ptile[...], ((0,), (0,))).astype(BF)
        w = slice(at, at + 2 * h)
        both = (
            dot(own, wgu[w, 0:H2], ((1,), (1,))) + dot(other, wgu[w, H2:2 * H2], ((1,), (1,)))
        ).astype(BF)
        for n in range(2):
            val = both[:, n * h:n * h + h]
            if (p, c) == (2, 1):
                val = jnp.concatenate([val, tiles[:, n * 128:n * 128 + 128]], axis=1)
            for b in range(4):
                rec[0][p][b * 192 + n * 96:b * 192 + n * 96 + 96, cols] = val[b * 96:b * 96 + 96, :]
        for by in (1, 3, 2):
            to = shifted(co, a3, by)
            send(
                rec[0][p].at[rows_at(to[a3] * 192, 192), cols],
                rrs[p].at[rows_at(co[a3] * 192, 192), cols],
                y_s.at[c, p, by - 1], y_r.at[c, p, by - 1], device(to, core),
            )
        mine = rows_at(co[a3] * 192, 192)
        rrs[p][mine, cols] = rec[0][p][mine, cols]

    for c in range(2):
        for p in range(3):
            input_part(p, c)
    send(delta_o, delta_out.at[CLASS:ROWS], h_s.at[0], h_r.at[0], partner)
    send(hid_o, hid.at[CLASS:ROWS], h_s.at[1], h_r.at[1], partner)
    c = pltpu.make_async_copy(delta, delta_out.at[0:CLASS], t_s.at[3])
    c.start()
    stores.append(c)

    stage_d = (rg0.at[0:CLASS, 0:STEP], rg0.at[CLASS:ROWS, 0:STEP])

    def down_out_copy(n, cols):
        return pltpu.make_async_copy(stage_d[n], down_out.at[0, :, cols], o_s.at[n])

    def down_step(i, carry):
        for n in range(2):
            @pl.when(i > 0)
            def _():
                down_out_copy(n, slice(0, STEP)).wait()
            cols = pl.ds(pl.multiple_of((2 * i + n) * STEP, STEP), STEP)
            stage_d[n][...] = dot(hid[...], rows_g[:, cols], ((0,), (0,))).astype(BF)
            down_out_copy(n, cols).start()
        return carry

    sums = gts

    def relay(c):
        for p, (a1, a2, a3) in enumerate(ORDERS):
            cols = piece(p, c)[2]
            for by in (1, 3, 2):
                ref = rrs[p].at[rows_at(lax.rem(co[a3] + 4 - by, 4) * 192, 192), cols]
                arrive(ref, y_s.at[c, p, by - 1], y_r.at[c, p, by - 1])
            sums[p][:, cols] = dot(ggs[p][...], rrs[p][:, cols]).astype(BF)
            for by in (1, 3, 2):
                to = shifted(co, a2, by)
                send(
                    sums[p].at[rows_at(to[a2] * LINE, LINE), cols], bss[p].at[by - 1, :, cols],
                    b2_s.at[c, p, by - 1], b2_r.at[c, p, by - 1], device(to, core),
                )

    def line_sum(c):
        for p, (a1, a2, a3) in enumerate(ORDERS):
            cols = piece(p, c)[2]
            total = sums[p][rows_at(co[a2] * LINE, LINE), cols].astype(F32)
            for by in (1, 3, 2):
                arrive(bss[p].at[by - 1, :, cols], b2_s.at[c, p, by - 1], b2_r.at[c, p, by - 1])
                total = total + bss[p][by - 1, :, cols].astype(F32)
            uss[p][:, cols] = total.astype(BF)
            for by in (1, 3, 2):
                to = shifted(co, a1, by)
                send(
                    uss[p].at[rows_at(to[a1] * BLOCK, BLOCK), cols], css[p].at[by - 1, :, cols],
                    b1_s.at[c, p, by - 1], b1_r.at[c, p, by - 1], device(to, core),
                )

    def finish(c):
        for p, (a1, a2, a3) in enumerate(ORDERS):
            at, h, cols = piece(p, c)
            total = uss[p][rows_at(co[a1] * BLOCK, BLOCK), cols].astype(F32)
            for by in (1, 3, 2):
                arrive(css[p].at[by - 1, :, cols], b1_s.at[c, p, by - 1], b1_r.at[c, p, by - 1])
                total = total + css[p][by - 1, :, cols].astype(F32)
            token_grad[:, at:at + h] = total[0:TOK, 0:h].astype(BF)
            token_grad[:, at + h:at + 2 * h] = total[TOK:, 0:h].astype(BF)
            if (p, c) == (2, 1):
                per = total[0:TOK, h:h + 128] + total[TOK:, h:h + 128]
                lane = lax.broadcasted_iota(jnp.int32, (TOK, 128), 1).astype(F32)
                spot = lax.broadcasted_iota(jnp.int32, (TOK, TOP), 1)
                grad = jnp.zeros((TOK, TOP), F32)
                for k in range(TOP):
                    one = jnp.sum(
                        jnp.where(lane == routes[:, k:k + 1], per, 0.0), axis=1, keepdims=True
                    )
                    grad = jnp.where(spot == k, one, grad)
                prob_grad[...] = lax.dot_general(
                    unit(TOP, F32), grad, (((1,), (1,)), ((), ())),
                    preferred_element_type=F32, precision=lax.Precision.HIGHEST,
                )

    relay(0)
    for p in range(3):
        cols = slice(G_AT[p], G_AT[p] + 2 * G_HALF[p])
        arrive(rows_g.at[CLASS:ROWS, cols], d_s.at[1, p], d_r.at[1, p])
    arrive(hid.at[CLASS:ROWS], h_s.at[1], h_r.at[1])
    lax.fori_loop(0, 2, down_step, 0)
    relay(1)
    line_sum(0)
    lax.fori_loop(2, 4, down_step, 0)
    line_sum(1)
    finish(0)
    finish(1)
    for n in range(2):
        down_out_copy(n, slice(0, STEP)).wait()
    for p in range(3):
        cols = slice(T_AT[p], T_AT[p] + 2 * T_HALF[p])
        arrive(rows_out.at[CLASS:ROWS, cols], d_s.at[0, p], d_r.at[0, p])
    arrive(delta_out.at[CLASS:ROWS], h_s.at[0], h_r.at[0])
    for c in stores:
        c.wait()
    for c in weights:
        c.wait_send()
    settle()


def weight_kernel(
    token, prob, rows, delta, down, token_out, prob_out, gate_out, up_out, down_out, held, i_s, o_s
):
    step = pl.program_id(0)
    quarters = [slice(n * SLOTS, n * SLOTS + SLOTS) for n in range(4)]
    ins = [
        pltpu.make_async_copy(down.at[0, part], held.at[part], i_s.at[n])
        for n, part in enumerate(quarters)
    ]
    outs = [
        pltpu.make_async_copy(held.at[part], down_out.at[0, part], o_s.at[n])
        for n, part in enumerate(quarters)
    ]

    @pl.when(step == 0)
    def _():
        for c in ins:
            c.start()
        token_out[...] = token[...]
        prob_out[...] = prob[...]

    grads = dot(rows[...], delta[...], ((0,), (0,))).astype(BF)
    gate_out[0] = grads[:, 0:HALF]
    up_out[0] = grads[:, HALF:2 * HALF]

    @pl.when(step == 1)
    def _():
        for c, d in zip(ins, outs):
            c.wait()
            d.start()

    @pl.when(step == D // TALL - 1)
    def _():
        for d in outs:
            d.wait()


def on_device(tokens, out_grad, routes, gate_probs, gate_weight, up_weight, down_weight):
    vmem = pl.BlockSpec(memory_space=pltpu.VMEM)
    anywhere = pl.BlockSpec(memory_space=pl.ANY)
    dma = pltpu.SemaphoreType.DMA
    shapes = [(CLASS, D), (ROWS, D), (D, 4 * HALF), (2 * HALF, D)]
    shapes += [(PLANE, 896), (PLANE, 768), (PLANE, 768)] + [(PLANE, 768)] * 3
    shapes += [(576, w) for w in T_SENT] + [(576, w) for w in G_HALF]
    shapes += [(ROWS, w) for w in T_SENT] + [(ROWS, w) for w in (640, 768, 768)]
    shapes += [(ROWS, w) for w in BACK]
    shapes += [(3, LINE, w) for w in BACK]
    shapes += [(3, BLOCK, w) for w in BACK]
    shapes += [PERM.shape, (CLASS, 2 * HALF), (ROWS, HALF)]
    scratch = [pltpu.VMEM(s, BF) for s in shapes] + [pltpu.VMEM((CLASS, 4 * HALF), F32)]
    for s in ((2, 3, 3), (2, 3, 6), (2, 3, 3), (2, 3), (3,), (2,)) + ((2, 3, 3),) * 3:
        scratch += [dma(s), dma(s)]
    scratch += [dma((4,)), dma((2,)), dma((4,))]
    token_shape = jax.ShapeDtypeStruct((TOK, D), BF)
    prob_shape = jax.ShapeDtypeStruct((TOP, TOK), F32)
    wide_shape = jax.ShapeDtypeStruct((1, D, HALF), BF)
    down_shape = jax.ShapeDtypeStruct((1, HALF, D), BF)
    results = pl.pallas_call(
        kernel,
        out_shape=(
            token_shape,
            prob_shape,
            jax.ShapeDtypeStruct((ROWS, D), BF),
            jax.ShapeDtypeStruct((ROWS, 2 * HALF), BF),
            down_shape,
        ),
        in_specs=[vmem] * 4 + [anywhere] * 4,
        out_specs=(vmem, vmem, anywhere, anywhere, anywhere),
        scratch_shapes=scratch,
        compiler_params=pltpu.CompilerParams(
            collective_id=1, has_side_effects=True, vmem_limit_bytes=65400 * 2**10
        ),
        name="routed_backward",
    )(
        tokens, out_grad, routes.T, gate_probs.T, jnp.asarray(PERM, BF),
        gate_weight, up_weight, down_weight,
    )
    whole = [pl.BlockSpec((TOK, D), lambda i: (0, 0)), pl.BlockSpec((TOP, TOK), lambda i: (0, 0))]
    tall = pl.BlockSpec((1, TALL, HALF), lambda i: (0, i, 0))
    token_grad, prob_grad, gate_grad, up_grad, down_grad = pl.pallas_call(
        weight_kernel,
        grid=(D // TALL,),
        out_shape=(token_shape, prob_shape, wide_shape, wide_shape, down_shape),
        in_specs=whole + [
            pl.BlockSpec((ROWS, TALL), lambda i: (0, i)),
            pl.BlockSpec((ROWS, 2 * HALF), lambda i: (0, 0)),
            anywhere,
        ],
        out_specs=whole + [tall, tall, anywhere],
        scratch_shapes=[pltpu.VMEM((HALF, D), BF), dma((4,)), dma((4,))],
        compiler_params=pltpu.CompilerParams(vmem_limit_bytes=62 * 2**20),
        name="weight_grads",
    )(*results)
    return token_grad, prob_grad.T, gate_grad, up_grad, down_grad


def solution(mesh):
    two, three = P(("dp", "expert"), None), P(("dp", "expert"), None, None)
    return jax.shard_map(
        on_device,
        mesh=mesh,
        in_specs=(two, two, two, two, three, three, three),
        out_specs=(two, two, three, three, three),
        check_vma=False,
    )
```
